32 devices in a mesh: dp: 8 (over y, x, core), mp: 4 (over z).
Axes of the slice: x: 2, y: 2, z: 4, core: 2. Of those that a mesh axis runs over, the one named last changes fastest.
Arguments:
- tokens: int32 [8192], P('dp'), may hold values from 0 to 31999
- targets: int32 [8192], P('dp'), may hold values from 0 to 31999
- select: int32 [8192], P('dp'), may hold values from 0 to 1
- bucket: int32 [8192], P('dp'), may hold values from 1 to 4
- embed_table: float32 [32000, 2048], P('mp', 'dp'), may hold values from -6 to 6
- query_weight: float32 [2048, 2048], P('dp', 'mp'), may hold values from -0.125 to 0.125
- keyvalue_weight: float32 [2048, 512], P('dp'), may hold values from -0.125 to 0.125
- output_weight: float32 [2048, 2048], P('mp', 'dp'), may hold values from -0.5 to 0.5
- gateup_weight: float32 [2, 2048, 5632], P(None, 'dp', 'mp'), may hold values from -0.125 to 0.125
- down_weight: float32 [5632, 2048], P('mp', 'dp'), may hold values from -0.078125 to 0.078125
- head_weight: float32 [2048, 32000], P('dp', 'mp'), may hold values from -0.22097087 to 0.22097087
- norm_gains: float32 [3, 2048], P(None, 'dp'), may hold values from 0.3 to 2.4
- embed_mean: float32 [32000, 2048], P('mp', 'dp'), may hold values from -4.7683716e-07 to 4.7683716e-07
- query_mean: float32 [2048, 2048], P('dp', 'mp'), may hold values from -4.7683716e-07 to 4.7683716e-07
- keyvalue_mean: float32 [2048, 512], P('dp'), may hold values from -4.7683716e-07 to 4.7683716e-07
- output_mean: float32 [2048, 2048], P('mp', 'dp'), may hold values from -4.7683716e-07 to 4.7683716e-07
- gateup_mean: float32 [2, 2048, 5632], P(None, 'dp', 'mp'), may hold values from -4.7683716e-07 to 4.7683716e-07
- down_mean: float32 [5632, 2048], P('mp', 'dp'), may hold values from -4.7683716e-07 to 4.7683716e-07
- head_mean: float32 [2048, 32000], P('dp', 'mp'), may hold values from -4.7683716e-07 to 4.7683716e-07
- gains_mean: float32 [3, 2048], P(None, 'dp'), may hold values from -4.7683716e-06 to 4.7683716e-06
- embed_square: float32 [32000, 2048], P('mp', 'dp'), may hold values from 3.0036832e-14 to 1.1991891e-13
- query_square: float32 [2048, 2048], P('dp', 'mp'), may hold values from 3.0036832e-14 to 1.1991891e-13
- keyvalue_square: float32 [2048, 512], P('dp'), may hold values from 3.0036832e-14 to 1.1991891e-13
- output_square: float32 [2048, 2048], P('mp', 'dp'), may hold values from 3.0036832e-14 to 1.1991891e-13
- gateup_square: float32 [2, 2048, 5632], P(None, 'dp', 'mp'), may hold values from 3.0036832e-14 to 1.1991891e-13
- down_square: float32 [5632, 2048], P('mp', 'dp'), may hold values from 3.0036832e-14 to 1.1991891e-13
- head_square: float32 [2048, 32000], P('dp', 'mp'), may hold values from 1.1991891e-13 to 4.7967565e-13
- gains_square: float32 [3, 2048], P(None, 'dp'), may hold values from 3.0036832e-12 to 1.1991891e-11
Outputs:
- loss_sum: float32 [], replicated
- weight_total: float32 [], replicated
- grad_norm: float32 [], replicated
- embed_final: float32 [32000, 2048], P('mp', 'dp')
- embed_clipped: float32 [32000, 2048], P('mp', 'dp')
- embed_square_out: float32 [32000, 2048], P('mp', 'dp')
- query_final: float32 [2048, 2048], P('dp', 'mp')
- query_mean_out: float32 [2048, 2048], P('dp', 'mp')
- query_square_out: float32 [2048, 2048], P('dp', 'mp')
- keyvalue_final: float32 [2048, 512], P('dp')
- keyvalue_mean_out: float32 [2048, 512], P('dp')
- keyvalue_square_out: float32 [2048, 512], P('dp')
- output_final: float32 [2048, 2048], P('mp', 'dp')
- output_mean_out: float32 [2048, 2048], P('mp', 'dp')
- output_square_out: float32 [2048, 2048], P('mp', 'dp')
- gateup_final: float32 [2, 2048, 5632], P(None, 'dp', 'mp')
- gateup_mean_out: float32 [2, 2048, 5632], P(None, 'dp', 'mp')
- gateup_square_out: float32 [2, 2048, 5632], P(None, 'dp', 'mp')
- down_final: float32 [5632, 2048], P('mp', 'dp')
- down_mean_out: float32 [5632, 2048], P('mp', 'dp')
- down_square_out: float32 [5632, 2048], P('mp', 'dp')
- head_final: float32 [2048, 32000], P('dp', 'mp')
- head_mean_out: float32 [2048, 32000], P('dp', 'mp')
- head_square_out: float32 [2048, 32000], P('dp', 'mp')
- gains_final: float32 [3, 2048], P(None, 'dp')
- gains_mean_out: float32 [3, 2048], P(None, 'dp')
- gains_square_out: float32 [3, 2048], P(None, 'dp')
The draws below stay inside these ranges and needn't reach their ends.
All inputs are finite; a program needn't handle non-finite values.
Results may differ from the reference program's by a relative error of at most 0.023.
Values may be sent and summed in bfloat16 or wider, within the bound.
No kernel may reach another device: no remote copies, remote signals or barrier semaphores. Data moves between devices by JAX's collectives and lax.ppermute only.
A program may use at most 448 MiB of HBM per device.

```python
import math
import jax
import jax.numpy as jnp
import numpy as np
from jax import lax

D = 2048
H = 32
HD = 64
KVH = 4
FF = 5632
V = 32000
LEN = 1024
STEP = 5
SEQS = 8
TOKENS = 8192
PARAMS = 175118336
N_MP = 4


def draw_select(key, part):
    key = jax.random.fold_in(key, 1)
    places = jnp.arange(TOKENS, dtype=jnp.int32)
    limit = 250 + 500 * places // TOKENS
    drawn = jax.random.randint(key, (TOKENS,), 0, 1000, dtype=jnp.int32)
    return (drawn < limit).astype(jnp.int32)


def draw_norm_gains(key, part):
    key = jax.random.fold_in(key, 2)
    ramp = jnp.arange(D, dtype=jnp.float32) / D
    noise = jax.random.uniform(key, (3, D), jnp.float32, 0.7, 1.3)
    return (0.5 + ramp)[None, :] * noise


def draw_head_weight(key, part):
    key = jax.random.fold_in(key, 3)
    column_key = jax.random.fold_in(key, 7)
    column_scale = jax.random.uniform(column_key, (1, V), jnp.float32, 0.8, 1.25)
    base = jax.random.truncated_normal(key, -3.0, 3.0, (D, V), jnp.float32) * 2.6
    return base * column_scale * D ** (-0.5)


def with_ends(array, own_key, least, top_value):
    place = [jax.random.randint(jax.random.fold_in(own_key, axis), (), 0, length) for axis, length in enumerate(array.shape)]
    longest = array.shape.index(max(array.shape))
    next_to = place[:longest] + [(place[longest] + 1) % array.shape[longest]] + place[longest + 1:]
    return array.at[tuple(place)].set(least).at[tuple(next_to)].set(top_value)


def block_scale(rng, extent, cuts, least, top_value):
    level, own = 1.0, jax.random.fold_in(rng, 6)
    for dim, blocks in cuts:
        steps = jnp.exp(jax.random.uniform(jax.random.fold_in(own, dim), (blocks,), jnp.float32, least / len(cuts), top_value / len(cuts)))
        level = level * jnp.repeat(steps, extent[dim] // blocks).reshape([-1 if axis == dim else 1 for axis in range(len(extent))])
    return level


def rank_bounds(count, skew):
    weights = [(1 << 20) // math.isqrt(standing ** skew) + 1 for standing in range(1, count + 1)]
    spread = 1 + sum(weights) // (1 << 30)
    return np.cumsum(np.array([max(1, weight // spread) for weight in weights]))


def ranked(stream_key, extent, amount, slope):
    listing = rank_bounds(amount, slope)
    pick = jax.random.randint(jax.random.fold_in(stream_key, 1), extent, 0, int(listing[amount - 1]))
    standing = jnp.searchsorted(jnp.asarray(listing, jnp.int32), pick, side="right")
    return jax.random.permutation(jax.random.fold_in(stream_key, 2), amount)[standing].astype(jnp.int32)


def bell_draw(key, dims, scale, reach, cuts=(), held_as=jnp.bfloat16):
    values = scale * jax.random.normal(key, dims, jnp.float32)
    if cuts:
        values = values * block_scale(key, dims, cuts, -0.22, 0.18)
    return jnp.clip(values, -reach, reach).astype(held_as)


def setup_inputs(seed: int = 0) -> dict:
    seeds = jax.random.split(jax.random.key(seed), 29)
    tokens = with_ends(ranked(seeds[0], (TOKENS,), V, 2), jax.random.fold_in(seeds[0], 3), 0, V - 1).astype(jnp.int32)
    targets = with_ends(ranked(seeds[1], (TOKENS,), V, 2), jax.random.fold_in(seeds[1], 3), 0, V - 1).astype(jnp.int32)
    select = draw_select(jax.random.fold_in(seeds[28], 71), 0)
    bucket = with_ends(jax.random.randint(seeds[3], (TOKENS,), 1, 5), jax.random.fold_in(seeds[3], 1), 1, 4).astype(jnp.int32)
    embed_table = bell_draw(seeds[4], (V, D), 1.0, 6.0, ((0, 4), (1, 8)), jnp.float32)
    query_weight = bell_draw(seeds[5], (D, H * HD), D ** -0.5, 0.125, ((0, 8), (1, 4)), jnp.float32)
    keyvalue_weight = bell_draw(seeds[6], (D, 2 * KVH * HD), D ** -0.5, 0.125, ((0, 8),), jnp.float32)
    output_weight = bell_draw(seeds[7], (H * HD, D), (H * HD // 16) ** -0.5, 0.5, ((0, 4), (1, 8)), jnp.float32)
    gateup_weight = bell_draw(seeds[8], (2, D, FF), D ** -0.5, 0.125, ((1, 8), (2, 4)), jnp.float32)
    down_weight = bell_draw(seeds[9], (FF, D), FF ** -0.5, 0.078125, ((0, 4), (1, 8)), jnp.float32)
    head_weight = draw_head_weight(jax.random.fold_in(seeds[28], 71), 0)
    norm_gains = draw_norm_gains(jax.random.fold_in(seeds[28], 71), 0)
    embed_mean = bell_draw(seeds[12], (V, D), (0.00111 * PARAMS ** -0.5), 4.76837158203125e-07, ((0, 4), (1, 8)), jnp.float32)
    query_mean = bell_draw(seeds[13], (D, H * HD), (0.00111 * PARAMS ** -0.5), 4.76837158203125e-07, ((0, 8), (1, 4)), jnp.float32)
    keyvalue_mean = bell_draw(seeds[14], (D, 2 * KVH * HD), (0.00111 * PARAMS ** -0.5), 4.76837158203125e-07, ((0, 8),), jnp.float32)
    output_mean = bell_draw(seeds[15], (H * HD, D), (0.00111 * PARAMS ** -0.5), 4.76837158203125e-07, ((0, 4), (1, 8)), jnp.float32)
    gateup_mean = bell_draw(seeds[16], (2, D, FF), (0.00111 * PARAMS ** -0.5), 4.76837158203125e-07, ((1, 8), (2, 4)), jnp.float32)
    down_mean = bell_draw(seeds[17], (FF, D), (0.00111 * PARAMS ** -0.5), 4.76837158203125e-07, ((0, 4), (1, 8)), jnp.float32)
    head_mean = bell_draw(seeds[18], (D, V), (0.00111 * PARAMS ** -0.5), 4.76837158203125e-07, ((0, 8), (1, 4)), jnp.float32)
    gains_mean = bell_draw(seeds[19], (3, D), (0.0111 * PARAMS ** -0.5), 4.76837158203125e-06, ((1, 8),), jnp.float32)
    embed_square = jnp.clip(jnp.exp(math.log(1.1991891312422565e-13) - 1.3843914 * jax.random.uniform(seeds[20], (V, D), jnp.float32) ** block_scale(seeds[20], (V, D), ((0, 4), (1, 8)), -0.2, 0.2)), 3.003683185422851e-14, 1.1991891312422565e-13)
    query_square = jnp.clip(jnp.exp(math.log(1.1991891312422565e-13) - 1.3843914 * jax.random.uniform(seeds[21], (D, H * HD), jnp.float32) ** block_scale(seeds[21], (D, H * HD), ((0, 8), (1, 4)), -0.2, 0.2)), 3.003683185422851e-14, 1.1991891312422565e-13)
    keyvalue_square = jnp.clip(jnp.exp(math.log(1.1991891312422565e-13) - 1.3843914 * jax.random.uniform(seeds[22], (D, 2 * KVH * HD), jnp.float32) ** block_scale(seeds[22], (D, 2 * KVH * HD), ((0, 8),), -0.2, 0.2)), 3.003683185422851e-14, 1.1991891312422565e-13)
    output_square = jnp.clip(jnp.exp(math.log(1.1991891312422565e-13) - 1.3843914 * jax.random.uniform(seeds[23], (H * HD, D), jnp.float32) ** block_scale(seeds[23], (H * HD, D), ((0, 4), (1, 8)), -0.2, 0.2)), 3.003683185422851e-14, 1.1991891312422565e-13)
    gateup_square = jnp.clip(jnp.exp(math.log(1.1991891312422565e-13) - 1.3843914 * jax.random.uniform(seeds[24], (2, D, FF), jnp.float32) ** block_scale(seeds[24], (2, D, FF), ((1, 8), (2, 4)), -0.2, 0.2)), 3.003683185422851e-14, 1.1991891312422565e-13)
    down_square = jnp.clip(jnp.exp(math.log(1.1991891312422565e-13) - 1.3843914 * jax.random.uniform(seeds[25], (FF, D), jnp.float32) ** block_scale(seeds[25], (FF, D), ((0, 4), (1, 8)), -0.2, 0.2)), 3.003683185422851e-14, 1.1991891312422565e-13)
    head_square = jnp.clip(jnp.exp(math.log(4.796756524969026e-13) - 1.3862944 * jax.random.uniform(seeds[26], (D, V), jnp.float32) ** block_scale(seeds[26], (D, V), ((0, 8), (1, 4)), -0.2, 0.2)), 1.1991891312422565e-13, 4.796756524969026e-13)
    gains_square = jnp.clip(jnp.exp(math.log(1.1991890987161913e-11) - 1.3843914 * jax.random.uniform(seeds[27], (3, D), jnp.float32) ** block_scale(seeds[27], (3, D), ((1, 8),), -0.2, 0.2)), 3.0036832396329594e-12, 1.1991890987161913e-11)
    return dict(tokens=tokens, targets=targets, select=select, bucket=bucket, embed_table=embed_table, query_weight=query_weight, keyvalue_weight=keyvalue_weight, output_weight=output_weight, gateup_weight=gateup_weight, down_weight=down_weight, head_weight=head_weight, norm_gains=norm_gains, embed_mean=embed_mean, query_mean=query_mean, keyvalue_mean=keyvalue_mean, output_mean=output_mean, gateup_mean=gateup_mean, down_mean=down_mean, head_mean=head_mean, gains_mean=gains_mean, embed_square=embed_square, query_square=query_square, keyvalue_square=keyvalue_square, output_square=output_square, gateup_square=gateup_square, down_square=down_square, head_square=head_square, gains_square=gains_square)


@jax.custom_vjp
def low(v):
    return lax.optimization_barrier(v.astype(jnp.bfloat16)).astype(jnp.float32)

@jax.custom_vjp
def low_back(v):
    return v

def low_keep(v):
    return (low(v), None)

def low_pass(kept, grad):
    return (grad,)

def back_keep(v):
    return (v, None)

def back_low(kept, grad):
    return (low(grad),)
low.defvjp(low_keep, low_pass)
low_back.defvjp(back_keep, back_low)
EPS = 1e-05
SCALE = 0.125
CLIP = 0.01
BETA_ONE = 0.9
BETA_TWO = 0.95
ADAM_EPS = 1e-08
RATES = (0.9, 0.01, 0.01, 0.06, 0.01, 0.01, 0.08, 0.9)
DECAYS = (0.1, 0.1, 0.1, 0.1, 0.1, 0.1, 0.1, 0.0)
HIGH = lax.Precision.HIGHEST

def matmul(left, right):
    return jnp.dot(left, right, precision=HIGH, preferred_element_type=jnp.float32)

def rmsnorm(hidden, gain):
    return hidden * lax.rsqrt(lax.optimization_barrier(jnp.mean(hidden * hidden, axis=-1, keepdims=True)) + EPS) * gain

def rotary_tables(length):
    positions = (jnp.arange(length) % LEN).astype(jnp.float32)
    freqs = 10000.0 ** (-(2 * jnp.arange(HD // 2)).astype(jnp.float32) / HD)
    angles = positions[:, None] * freqs[None, :]
    cosine = jnp.cos(angles)
    sine = jnp.sin(angles)
    return (jnp.concatenate([cosine, cosine], -1), jnp.concatenate([sine, sine], -1))

def rotate(values, cosine, sine):
    half = HD // 2
    turned = jnp.concatenate([-values[..., half:], values[..., :half]], -1)
    return values * cosine[:, None, :] + turned * sine[:, None, :]

def group_columns():
    heads = np.arange(N_MP) * KVH // N_MP
    pieces = [np.concatenate([np.arange(HD) + c * HD, np.arange(HD) + (KVH + c) * HD]) for c in heads]
    return np.concatenate(pieces)

def sequence_loss(weights, ids, goals, scales):
    embed, query, keyvalue, output, gateup, down, head, gains = weights
    cosine, sine = rotary_tables(LEN)
    start = low_back(embed[ids])
    first = low(rmsnorm(start, gains[0]))
    queries = low(rotate(low_back(matmul(first, query)).reshape(LEN, H, HD), cosine, sine))
    pairs = low_back(matmul(first, keyvalue[:, group_columns()])).reshape(LEN, N_MP, 2, HD)
    keys = low(rotate(pairs[:, :, 0], cosine, sine))
    values = low(pairs[:, :, 1])
    grouped = queries.reshape(LEN, N_MP, H // N_MP, HD)
    scores = low_back(jnp.einsum('tgjd,sgd->gjts', grouped, keys, precision=HIGH) * SCALE)
    causal = jnp.arange(LEN)[:, None] >= jnp.arange(LEN)[None, :]
    probs = low(jax.nn.softmax(jnp.where(causal, scores, -1e+30), axis=-1))
    mixed = low(jnp.einsum('gjts,sgd->tgjd', probs, values, precision=HIGH)).reshape(LEN, H * HD)
    middle = start + low_back(matmul(mixed, output))
    second = low(rmsnorm(middle, gains[1]))
    gate = low_back(matmul(second, gateup[0]))
    upper = low_back(matmul(second, gateup[1]))
    active = low(jax.nn.silu(gate) * upper)
    final = middle + low_back(matmul(active, down))
    logits = low_back(matmul(low(rmsnorm(final, gains[2])), head))
    totals = jax.nn.logsumexp(logits, axis=-1)
    picked = jnp.take_along_axis(logits, goals[:, None], axis=-1)[:, 0]
    return jnp.sum(scales * (totals - picked))

def reference(tokens, targets, select, bucket, embed_table, query_weight, keyvalue_weight, output_weight, gateup_weight, down_weight, head_weight, norm_gains, embed_mean, query_mean, keyvalue_mean, output_mean, gateup_mean, down_mean, head_mean, gains_mean, embed_square, query_square, keyvalue_square, output_square, gateup_square, down_square, head_square, gains_square):
    params = tuple((w.astype(jnp.float32) for w in (embed_table, query_weight, keyvalue_weight, output_weight, gateup_weight, down_weight, head_weight, norm_gains)))
    means = (embed_mean, query_mean, keyvalue_mean, output_mean, gateup_mean, down_mean, head_mean, gains_mean)
    squares = (embed_square, query_square, keyvalue_square, output_square, gateup_square, down_square, head_square, gains_square)
    scales = (select * bucket).astype(jnp.float32)
    weight_total = jnp.sum(scales)
    shaped = (tokens.reshape(SEQS, LEN), targets.reshape(SEQS, LEN), scales.reshape(SEQS, LEN))

    def objective(weights):
        lowered = tuple((low(w) for w in weights))
        piece = jax.checkpoint(sequence_loss)

        def advance(carry, inputs):
            return (carry + piece(lowered, inputs[0], inputs[1], inputs[2]), None)
        total, _ = lax.scan(advance, jnp.zeros((), jnp.float32), shaped)
        return (total / weight_total, total)
    _, pullback, loss_sum = jax.vjp(objective, params, has_aux=True)
    grads = pullback(jnp.ones((), jnp.float32))[0]
    grad_norm = jnp.sqrt(sum((jnp.sum(piece * piece) for piece in grads)))
    factor = jnp.minimum(1.0, CLIP / (grad_norm + 1e-06))
    updates = []
    for number, (weight, grad, first_m, second_m, rate, decay) in enumerate(zip(params, grads, means, squares, RATES, DECAYS)):
        clipped = grad * factor
        mean_new = BETA_ONE * first_m + (1 - BETA_ONE) * clipped
        square_new = BETA_TWO * second_m + (1 - BETA_TWO) * clipped * clipped
        ratio = mean_new / (1 - BETA_ONE ** STEP) / (jnp.sqrt(square_new / (1 - BETA_TWO ** STEP)) + ADAM_EPS)
        updates += [weight - rate * (ratio + decay * weight), clipped if number == 0 else mean_new, square_new]
    return (loss_sum, weight_total, grad_norm, updates[0], updates[1], updates[2], updates[3], updates[4], updates[5], updates[6], updates[7], updates[8], updates[9], updates[10], updates[11], updates[12], updates[13], updates[14], updates[15], updates[16], updates[17], updates[18], updates[19], updates[20], updates[21], updates[22], updates[23])
```

```python
import functools

import jax
import jax.numpy as jnp
from jax import lax
from jax.experimental import pallas as pl
from jax.experimental.pallas import tpu as pltpu
from jax.sharding import PartitionSpec as P

HD = 64
KVH = 4
LEN = 1024
STEP = 5

EPS = 1e-05
SCALE = 0.125
CLIP = 0.01
BETA_ONE = 0.9
BETA_TWO = 0.95
ADAM_EPS = 1e-08
RATES = (0.9, 0.01, 0.01, 0.06, 0.01, 0.01, 0.08, 0.9)
DECAYS = (0.1, 0.1, 0.1, 0.1, 0.1, 0.1, 0.1, 0.0)

LANES = 128
QB = 256
VMEM_LIMIT = 56 * 1024 * 1024

f32 = jnp.float32
bf16 = jnp.bfloat16


def normed(hidden, gain):
    return hidden * lax.rsqrt(jnp.mean(hidden * hidden, axis=-1, keepdims=True) + EPS) * gain


def norm_back(hidden, gain, upstream):
    _, pullback = jax.vjp(normed, hidden, gain)
    return pullback(upstream)


def rotary_tables(length):
    positions = (jnp.arange(length) % LEN).astype(f32)
    freqs = 10000.0 ** (-(2 * jnp.arange(HD // 2)).astype(f32) / HD)
    angles = positions[:, None] * freqs[None, :]
    cosine = jnp.cos(angles)
    sine = jnp.sin(angles)
    return (
        jnp.concatenate([cosine] * 4, -1),
        jnp.concatenate([-sine, sine, -sine, sine], -1),
    )


def swap_halves(x, lane):
    half = HD // 2
    return jnp.where(
        lane % HD < half, pltpu.roll(x, LANES - half, 1), pltpu.roll(x, half, 1)
    )


def attend_kernel(q_ref, kv_ref, cos_ref, sin_ref, mixed_ref, rope_ref, key_ref, value_ref, lse_ref):
    rows = q_ref.shape[0]
    lane = lax.broadcasted_iota(jnp.int32, (rows, LANES), 1)
    cosine, sine = cos_ref[...], sin_ref[...]

    @pl.when(pl.program_id(0) == 0)
    def _():
        pair = kv_ref[...]
        other = pltpu.roll(pair, HD, 1)
        key = jnp.where(lane < HD, pair, other)
        value = jnp.where(lane < HD, other, pair)
        key_ref[...] = (key * cosine + swap_halves(key, lane) * sine).astype(bf16)
        value_ref[...] = value.astype(bf16)

    q = q_ref[...]
    rope_ref[...] = (q * cosine + swap_halves(q, lane) * sine).astype(bf16)
    low = lax.broadcasted_iota(jnp.int32, (QB, LANES), 1) < HD
    for block in range(rows // QB):
        at = block * QB
        width = at + QB
        chosen = rope_ref[at : at + QB, :]
        keys = key_ref[:width, :]
        values = value_ref[:width, :]
        places = at + lax.broadcasted_iota(jnp.int32, (QB, width), 0)
        causal = lax.broadcasted_iota(jnp.int32, (QB, width), 1) <= places
        outs, sums = [], []
        for part in range(2):
            mask = low if part == 0 else jnp.logical_not(low)
            one = jnp.where(mask, chosen, jnp.zeros_like(chosen))
            scores = SCALE * lax.dot_general(
                one, keys, (((1,), (1,)), ((), ())), preferred_element_type=f32
            )
            scores = jnp.where(causal, scores, -1e30)
            peak = jnp.max(scores, -1, keepdims=True)
            expo = jnp.exp(scores - peak)
            total = jnp.sum(expo, -1, keepdims=True)
            probs = (expo * (1.0 / total)).astype(bf16)
            outs.append(jnp.dot(probs, values, preferred_element_type=f32))
            sums.append(peak + jnp.log(total))
        mixed_ref[at : at + QB, :] = jnp.where(low, outs[0], outs[1]).astype(bf16)
        lse_ref[0, at : at + QB, :] = jnp.where(low, sums[0], sums[1])


def attend(qkv, cosine, sine):
    rows, cols = qkv.shape
    pairs = cols // LANES - 1
    whole = pl.BlockSpec((rows, LANES), lambda p: (0, 0))
    column = pl.BlockSpec((rows, LANES), lambda p: (0, p))
    return pl.pallas_call(
        attend_kernel,
        grid=(pairs,),
        in_specs=[column, pl.BlockSpec((rows, LANES), lambda p: (0, pairs)), whole, whole],
        out_specs=[column, column, whole, whole, pl.BlockSpec((1, rows, LANES), lambda p: (p, 0, 0))],
        out_shape=[
            jax.ShapeDtypeStruct((rows, pairs * LANES), bf16),
            jax.ShapeDtypeStruct((rows, pairs * LANES), bf16),
            jax.ShapeDtypeStruct((rows, LANES), bf16),
            jax.ShapeDtypeStruct((rows, LANES), bf16),
            jax.ShapeDtypeStruct((pairs, rows, LANES), f32),
        ],
        compiler_params=pltpu.CompilerParams(
            dimension_semantics=("arbitrary",), vmem_limit_bytes=VMEM_LIMIT
        ),
        name="attend",
    )(qkv, qkv, cosine, sine)


def attend_back_kernel(
    q_ref, key_ref, value_ref, lse_ref, grad_ref, cos_ref, sin_ref, dq_ref, dkv_ref, dk_acc, dv_acc
):
    rows = q_ref.shape[0]
    lane = lax.broadcasted_iota(jnp.int32, (rows, LANES), 1)
    step = pl.program_id(0)

    @pl.when(step == 0)
    def _():
        dk_acc[...] = jnp.zeros_like(dk_acc)
        dv_acc[...] = jnp.zeros_like(dv_acc)

    low = lax.broadcasted_iota(jnp.int32, (QB, LANES), 1) < HD
    lane_block = lax.broadcasted_iota(jnp.int32, (QB, LANES), 1)
    for block in range(rows // QB):
        at = block * QB
        width = at + QB
        chosen = q_ref[at : at + QB, :]
        upstream = grad_ref[at : at + QB, :]
        keys = key_ref[:width, :]
        values = value_ref[:width, :]
        places = at + lax.broadcasted_iota(jnp.int32, (QB, width), 0)
        causal = lax.broadcasted_iota(jnp.int32, (QB, width), 1) <= places
        outs = []
        for part in range(2):
            mask = low if part == 0 else jnp.logical_not(low)
            one = jnp.where(mask, chosen, jnp.zeros_like(chosen))
            grad = jnp.where(mask, upstream, jnp.zeros_like(upstream))
            scores = SCALE * lax.dot_general(
                one, keys, (((1,), (1,)), ((), ())), preferred_element_type=f32
            )
            lse = lse_ref[0, at : at + QB, part * HD : part * HD + 1]
            probs = jnp.where(causal, jnp.exp(scores - lse), 0.0)
            prob_grad = lax.dot_general(
                grad, values, (((1,), (1,)), ((), ())), preferred_element_type=f32
            )
            inner = jnp.sum(probs * prob_grad, -1, keepdims=True)
            score_grad = (probs * (prob_grad - inner)).astype(bf16)
            outs.append(jnp.dot(score_grad, keys, preferred_element_type=f32) * SCALE)
            dk_acc[:width, :] += SCALE * lax.dot_general(
                score_grad, one, (((0,), (0,)), ((), ())), preferred_element_type=f32
            )
            dv_acc[:width, :] += lax.dot_general(
                probs.astype(bf16), grad, (((0,), (0,)), ((), ())), preferred_element_type=f32
            )
        total = jnp.where(low, outs[0], outs[1])
        turned = swap_halves(total, lane_block)
        dq_ref[at : at + QB, :] = (
            total * cos_ref[at : at + QB, :] - turned * sin_ref[at : at + QB, :]
        ).astype(bf16)

    @pl.when(step == pl.num_programs(0) - 1)
    def _():
        dk = dk_acc[...]
        dk = dk + pltpu.roll(dk, HD, 1)
        dk = dk * cos_ref[...] - swap_halves(dk, lane) * sin_ref[...]
        dv = dv_acc[...]
        dv = dv + pltpu.roll(dv, HD, 1)
        dkv_ref[...] = jnp.where(lane < HD, dk, dv).astype(bf16)


def attend_back(rope, key, value, lse, grad, cosine, sine):
    rows, cols = rope.shape
    pairs = cols // LANES
    whole = pl.BlockSpec((rows, LANES), lambda p: (0, 0))
    column = pl.BlockSpec((rows, LANES), lambda p: (0, p))
    return pl.pallas_call(
        attend_back_kernel,
        grid=(pairs,),
        in_specs=[
            column,
            whole,
            whole,
            pl.BlockSpec((1, rows, LANES), lambda p: (p, 0, 0)),
            column,
            whole,
            whole,
        ],
        out_specs=[column, whole],
        out_shape=[
            jax.ShapeDtypeStruct((rows, cols), bf16),
            jax.ShapeDtypeStruct((rows, LANES), bf16),
        ],
        scratch_shapes=[pltpu.VMEM((rows, LANES), f32), pltpu.VMEM((rows, LANES), f32)],
        compiler_params=pltpu.CompilerParams(
            dimension_semantics=("arbitrary",), vmem_limit_bytes=VMEM_LIMIT
        ),
        name="attend_back",
    )(rope, key, value, lse, grad, cosine, sine)


def shift_up(x, size):
    return lax.ppermute(x, "mp", [(i, i + 1) for i in range(size - 1)])


def shift_down(x, size):
    return lax.ppermute(x, "mp", [(i + 1, i) for i in range(size - 1)])


def line_gather(shard):
    size = lax.axis_size("mp")
    me = lax.axis_index("mp")
    ups, downs = [shard], [shard]
    for _ in range(size - 1):
        ups.append(shift_up(ups[-1], size))
        downs.append(shift_down(downs[-1], size))
    whole = jnp.zeros((size,) + shard.shape, shard.dtype)
    whole = lax.dynamic_update_index_in_dim(whole, shard, me, 0)
    for hop in range(1, size):
        piece = jnp.where(me >= hop, ups[hop], downs[size - hop])
        whole = lax.dynamic_update_index_in_dim(whole, piece, (me - hop) % size, 0)
    return whole


def line_scatter(parts):
    size = parts.shape[0]
    me = lax.axis_index("mp")

    def own(place):
        return lax.dynamic_index_in_dim(parts, jnp.clip(place, 0, size - 1), 0, False)

    up, down = None, None
    for step in range(1, size):
        mine_up, mine_down = own(me + size - step), own(me - size + step)
        up = shift_up(mine_up if up is None else mine_up + up, size)
        down = shift_down(mine_down if down is None else mine_down + down, size)
    return own(me).astype(f32) + up.astype(f32) + down.astype(f32)


def spread(shard):
    whole = line_gather(shard)
    return whole.reshape(-1, shard.shape[-1])


def collect(partial_value):
    size = lax.axis_size("mp")
    return line_scatter(
        partial_value.astype(bf16).reshape(size, -1, partial_value.shape[-1])
    )


def adamw(weight, grad, mean_old, square_old, factor, rate, decay):
    clipped = grad.astype(f32) * factor
    mean_new = BETA_ONE * mean_old + (1 - BETA_ONE) * clipped
    square_new = BETA_TWO * square_old + (1 - BETA_TWO) * clipped * clipped
    ratio = (
        mean_new / (1 - BETA_ONE**STEP) / (jnp.sqrt(square_new / (1 - BETA_TWO**STEP)) + ADAM_EPS)
    )
    return (weight - rate * (ratio + decay * weight), mean_new, square_new)


def dot(a, b, dims=((1,), (0,)), out=f32):
    return lax.dot_general(a, b, (dims, ((), ())), preferred_element_type=f32).astype(out)


def body(
    tokens,
    targets,
    select,
    bucket,
    embed_table,
    query_weight,
    keyvalue_weight,
    output_weight,
    gateup_weight,
    down_weight,
    head_weight,
    norm_gains,
    embed_mean,
    query_mean,
    keyvalue_mean,
    output_mean,
    gateup_mean,
    down_mean,
    head_mean,
    gains_mean,
    embed_square,
    query_square,
    keyvalue_square,
    output_square,
    gateup_square,
    down_square,
    head_square,
    gains_square,
):
    n_dp, n_mp = lax.axis_size("dp"), lax.axis_size("mp")
    group = lax.axis_index("mp")
    rows = tokens.shape[0]
    home = rows // n_mp
    head_kv = group * KVH // n_mp
    embed_part_rows, embed_cols = embed_table.shape
    vocab_start = group * embed_part_rows
    q_cols = query_weight.shape[1]

    key_cols = lax.dynamic_slice_in_dim(keyvalue_weight, head_kv * HD, HD, 1)
    value_cols = lax.dynamic_slice_in_dim(keyvalue_weight, (KVH + head_kv) * HD, HD, 1)
    qkv_own = jnp.concatenate([query_weight, key_cols, value_cols], 1).astype(bf16)
    ids = lax.all_gather(tokens, "dp", axis=0, tiled=True)
    gains_rows = lax.all_gather(norm_gains.astype(bf16), "dp", axis=1, tiled=True).astype(f32)
    qkv_full = lax.all_gather(qkv_own, "dp", axis=0, tiled=True)
    output_full = lax.all_gather(output_weight.astype(bf16), "dp", axis=1, tiled=True)
    gateup_full = lax.all_gather(gateup_weight.astype(bf16), "dp", axis=1, tiled=True)
    down_full = lax.all_gather(down_weight.astype(bf16), "dp", axis=1, tiled=True)
    head_full = lax.all_gather(head_weight.astype(bf16), "dp", axis=0, tiled=True)
    cosine, sine = rotary_tables(rows)

    ids_local = ids - vocab_start
    inside = (ids_local >= 0) & (ids_local < embed_part_rows)
    looked = embed_table[jnp.clip(ids_local, 0, embed_part_rows - 1)]
    looked = jnp.where(inside[:, None], looked, 0.0).astype(bf16)
    looked = looked.reshape(n_dp, n_mp, home, embed_cols).transpose(1, 0, 2, 3)
    looked = line_scatter(looked.reshape(n_mp, n_dp * home, embed_cols)).astype(bf16)
    looked = lax.all_to_all(looked.reshape(n_dp, home, embed_cols), "dp", 0, 0)
    start_rows = looked.transpose(1, 0, 2).reshape(home, -1).astype(f32)

    first_in = spread(normed(start_rows, gains_rows[0]).astype(bf16))
    qkv = dot(first_in, qkv_full)
    mixed, rope, key, value, lse = attend(qkv, cosine, sine)
    middle_rows = start_rows + collect(dot(mixed, output_full, out=bf16))
    second_in = spread(normed(middle_rows, gains_rows[1]).astype(bf16))
    gate = dot(second_in, gateup_full[0])
    upper = dot(second_in, gateup_full[1])
    active = (jax.nn.silu(gate) * upper).astype(bf16)
    final_rows = middle_rows + collect(dot(active, down_full, out=bf16))
    final_in = spread(normed(final_rows, gains_rows[2]).astype(bf16))
    logits = dot(final_in, head_full)
    hits = jnp.arange(head_full.shape[1])[None, :] == (targets - group * head_full.shape[1])[:, None]
    local_top = jnp.max(logits, -1)
    stats = lax.all_gather(
        jnp.stack(
            [
                local_top,
                jnp.sum(jnp.exp(logits - local_top[:, None]), -1),
                jnp.sum(jnp.where(hits, logits, 0.0), -1),
            ]
        ),
        "mp",
    )
    top = jnp.max(stats[:, 0], 0)
    expsum = jnp.sum(stats[:, 1] * jnp.exp(stats[:, 0] - top[None]), 0)
    logsum_all = top + jnp.log(expsum)
    picked = jnp.sum(stats[:, 2], 0)
    scales = (select * bucket).astype(f32)
    loss_sum, weight_total = lax.psum(
        (jnp.sum(scales * (logsum_all - picked)), jnp.sum(scales)), "dp"
    )
    coef = scales * (1.0 / weight_total)
    logit_grad = (
        (jnp.exp(logits - logsum_all[:, None]) - hits.astype(f32)) * coef[:, None]
    ).astype(bf16)

    def reduce_rows(grad):
        return lax.psum_scatter(grad, "dp", scatter_dimension=0, tiled=True)

    final_partial = dot(logit_grad, head_full, ((1,), (1,)), bf16)
    head_part = reduce_rows(dot(final_in, logit_grad, ((0,), (0,)), bf16))
    final_grad = collect(final_partial)
    residual, final_gain = norm_back(final_rows, gains_rows[2], final_grad)
    branch = spread(residual.astype(bf16))
    sigmoid = jax.nn.sigmoid(gate)
    silu_gate = gate * sigmoid
    active_grad = dot(branch, down_full, ((1,), (1,)))
    gate_grad = (active_grad * upper * sigmoid * (1.0 + gate * (1.0 - sigmoid))).astype(bf16)
    upper_grad = (active_grad * silu_gate).astype(bf16)
    second_partial = (
        dot(gate_grad, gateup_full[0], ((1,), (1,)))
        + dot(upper_grad, gateup_full[1], ((1,), (1,)))
    ).astype(bf16)
    down_part = lax.psum_scatter(
        dot(active, branch, ((0,), (0,)), bf16), "dp", scatter_dimension=1, tiled=True
    )
    gateup_part = lax.psum_scatter(
        jnp.stack(
            [
                dot(second_in, gate_grad, ((0,), (0,)), bf16),
                dot(second_in, upper_grad, ((0,), (0,)), bf16),
            ]
        ),
        "dp",
        scatter_dimension=1,
        tiled=True,
    )
    second_grad = collect(second_partial)
    middle_extra, middle_gain = norm_back(middle_rows, gains_rows[1], second_grad)
    residual = residual + middle_extra
    branch = spread(residual.astype(bf16))
    mixed_grad = dot(branch, output_full, ((1,), (1,)), bf16)
    query_pre, pair_grad = attend_back(rope, key, value, lse, mixed_grad, cosine, sine)
    output_part = lax.psum_scatter(
        dot(mixed, branch, ((0,), (0,)), bf16), "dp", scatter_dimension=1, tiled=True
    )
    qkv_grad = jnp.concatenate([query_pre, pair_grad], 1)
    first_grad = collect(dot(qkv_grad, qkv_full, ((1,), (1,)), bf16))
    start_extra, start_gain = norm_back(start_rows, gains_rows[0], first_grad)
    start_grad = (residual + start_extra).astype(bf16)
    gains_grad = jnp.stack([start_gain, middle_gain, final_gain], 1).astype(bf16)
    small = reduce_rows(
        jnp.concatenate([dot(first_in, qkv_grad, ((0,), (0,)), bf16), gains_grad], 1)
    )
    query_part = small[:, :q_cols]

    moved = start_grad.reshape(home, n_dp, embed_cols).transpose(1, 0, 2)
    moved = lax.all_to_all(moved, "dp", 0, 0)
    moved = spread(moved.reshape(n_dp * home, embed_cols))
    moved_ids = ids_local.reshape(n_dp, n_mp, home).transpose(1, 0, 2).reshape(-1)
    onehot_back = (moved_ids[None, :] == jnp.arange(embed_part_rows)[:, None]).astype(bf16)
    embed_part = dot(onehot_back, moved)

    shared = lax.all_gather(small[:, q_cols:], "mp").astype(f32)
    gains_part = jnp.sum(shared[:, :, 2 * HD :], 0).T
    keyvalue_part = jnp.zeros(keyvalue_weight.shape, f32)
    for source in range(n_mp):
        c = source * KVH // n_mp
        keyvalue_part = keyvalue_part.at[:, c * HD : (c + 1) * HD].add(shared[source, :, :HD])
        keyvalue_part = keyvalue_part.at[:, (KVH + c) * HD : (KVH + c + 1) * HD].add(
            shared[source, :, HD : 2 * HD]
        )

    leading = (group == 0).astype(f32)

    def square(piece):
        piece = piece.astype(f32)
        return jnp.sum(piece * piece)

    squared = sum(
        square(piece)
        for piece in (embed_part, query_part, output_part, gateup_part, down_part, head_part)
    )
    squared = squared + leading * (square(keyvalue_part) + square(gains_part))
    grad_norm = jnp.sqrt(lax.psum(squared, ("dp", "mp")))
    factor = jnp.minimum(1.0, CLIP / (grad_norm + 1e-06))
    outs = [loss_sum, weight_total, grad_norm]
    for number, (weight, grad, mean_old, square_old) in enumerate(
        (
            (embed_table, embed_part, embed_mean, embed_square),
            (query_weight, query_part, query_mean, query_square),
            (keyvalue_weight, keyvalue_part, keyvalue_mean, keyvalue_square),
            (output_weight, output_part, output_mean, output_square),
            (gateup_weight, gateup_part, gateup_mean, gateup_square),
            (down_weight, down_part, down_mean, down_square),
            (head_weight, head_part, head_mean, head_square),
            (norm_gains, gains_part, gains_mean, gains_square),
        )
    ):
        new, mean_new, square_new = adamw(
            weight, grad, mean_old, square_old, factor, RATES[number], DECAYS[number]
        )
        outs += [new, embed_part * factor if number == 0 else mean_new, square_new]
    return tuple(outs)


def solution(mesh):
    weights = (
        P("mp", "dp"),
        P("dp", "mp"),
        P("dp", None),
        P("mp", "dp"),
        P(None, "dp", "mp"),
        P("mp", "dp"),
        P("dp", "mp"),
        P(None, "dp"),
    )
    in_specs = (P("dp"),) * 4 + weights * 3
    out_specs = (P(),) * 3 + tuple(spec for spec in weights for _ in range(3))
    return jax.shard_map(body, mesh=mesh, in_specs=in_specs, out_specs=out_specs, check_vma=False)
```

```python
import functools

import jax
import jax.numpy as jnp
from jax import lax
from jax.experimental import pallas as pl
from jax.experimental.pallas import tpu as pltpu
from jax.sharding import PartitionSpec as P

HD = 64
KVH = 4
LEN = 1024
STEP = 5

EPS = 1e-05
SCALE = 0.125
CLIP = 0.01
BETA_ONE = 0.9
BETA_TWO = 0.95
ADAM_EPS = 1e-08
RATES = (0.9, 0.01, 0.01, 0.06, 0.01, 0.01, 0.08, 0.9)
DECAYS = (0.1, 0.1, 0.1, 0.1, 0.1, 0.1, 0.1, 0.0)

LANES = 128
VMEM_LIMIT = 56 * 1024 * 1024

f32 = jnp.float32
bf16 = jnp.bfloat16


def normed(hidden, gain):
    return hidden * lax.rsqrt(jnp.mean(hidden * hidden, axis=-1, keepdims=True) + EPS) * gain


def norm_back(hidden, gain, upstream):
    _, pullback = jax.vjp(normed, hidden, gain)
    return pullback(upstream)


def rotary_tables(places):
    freqs = 10000.0 ** (-(2 * jnp.arange(HD // 2)).astype(f32) / HD)
    angles = (places % LEN).astype(f32)[:, None] * freqs[None, :]
    cosine = jnp.cos(angles)
    sine = jnp.sin(angles)
    return (
        jnp.concatenate([cosine] * 4, -1),
        jnp.concatenate([-sine, sine, -sine, sine], -1),
    )


def swap_halves(x, lane):
    half = HD // 2
    return jnp.where(
        lane % HD < half, pltpu.roll(x, LANES - half, 1), pltpu.roll(x, half, 1)
    )


def lanes_of(shape):
    return lax.broadcasted_iota(jnp.int32, shape, 1)


def turn_kernel(sign, kv_ref, cos_ref, sin_ref, out_ref):
    rows = kv_ref.shape[0]
    lane = lanes_of((rows, LANES))
    x = kv_ref[...]
    turned = x * cos_ref[...] + sign * swap_halves(x, lane) * sin_ref[...]
    out_ref[...] = jnp.where(lane < HD, turned, x).astype(bf16)


def turn_keys(kv, cosine, sine, sign, n_heads):
    rows = kv.shape[0]
    column = pl.BlockSpec((rows, LANES), lambda p: (0, p))
    whole = pl.BlockSpec((rows, LANES), lambda p: (0, 0))
    return pl.pallas_call(
        functools.partial(turn_kernel, sign),
        grid=(n_heads,),
        in_specs=[column, whole, whole],
        out_specs=column,
        out_shape=jax.ShapeDtypeStruct((rows, n_heads * LANES), bf16),
        name="turn_keys",
    )(kv, cosine, sine)


def load_keys(step, per_head, kv_ref, key_ref, value_ref):
    @pl.when(step % per_head == 0)
    def _():
        pair = kv_ref[...].astype(f32)
        other = pltpu.roll(pair, HD, 1)
        lane = lanes_of(pair.shape)
        key_ref[...] = jnp.where(lane < HD, pair, other).astype(bf16)
        value_ref[...] = jnp.where(lane < HD, other, pair).astype(bf16)


def attend_kernel(
    per_head, q_ref, kv_ref, cos_ref, sin_ref, place_ref, key_place_ref,
    mixed_ref, rope_ref, lse_ref, key_ref, value_ref,
):
    rows = q_ref.shape[0]
    half_rows, n_keys = rows // 2, kv_ref.shape[0]
    load_keys(pl.program_id(0), per_head, kv_ref, key_ref, value_ref)
    q = q_ref[...]
    rope_ref[...] = (q * cos_ref[...] + swap_halves(q, lanes_of(q.shape)) * sin_ref[...]).astype(bf16)
    low = lanes_of((half_rows, LANES)) < HD
    for block in range(2):
        at, width = block * half_rows, (block + 1) * n_keys // 2
        chosen = rope_ref[at : at + half_rows, :]
        keys, values = key_ref[:width, :], value_ref[:width, :]
        causal = key_place_ref[:, :width] <= place_ref[at : at + half_rows, :]
        outs, sums = [], []
        for part in range(2):
            mask = low if part == 0 else jnp.logical_not(low)
            one = jnp.where(mask, chosen, jnp.zeros_like(chosen))
            scores = SCALE * lax.dot_general(
                one, keys, (((1,), (1,)), ((), ())), preferred_element_type=f32
            )
            scores = jnp.where(causal, scores, -1e30)
            peak = jnp.max(scores, -1, keepdims=True)
            expo = jnp.exp(scores - peak)
            total = jnp.sum(expo, -1, keepdims=True)
            probs = (expo * (1.0 / total)).astype(bf16)
            outs.append(jnp.dot(probs, values, preferred_element_type=f32))
            sums.append(peak + jnp.log(total))
        mixed_ref[at : at + half_rows, :] = jnp.where(low, outs[0], outs[1]).astype(bf16)
        lse_ref[0, at : at + half_rows, :] = jnp.where(low, sums[0], sums[1])


def attend(kvq, kv, cosine, sine, places, key_places):
    rows, cols = kvq.shape
    n_keys, kv_cols = kv.shape
    pairs, kv_heads = (cols - kv_cols) // LANES, kv_cols // LANES
    per_head = pairs // kv_heads
    whole = pl.BlockSpec((rows, LANES), lambda p: (0, 0))
    column = pl.BlockSpec((rows, LANES), lambda p: (0, p))
    return pl.pallas_call(
        functools.partial(attend_kernel, per_head),
        grid=(pairs,),
        in_specs=[
            pl.BlockSpec((rows, LANES), lambda p: (0, p + kv_heads)),
            pl.BlockSpec((n_keys, LANES), lambda p: (0, p // per_head)),
            whole,
            whole,
            pl.BlockSpec((rows, 1), lambda p: (0, 0)),
            pl.BlockSpec((1, n_keys), lambda p: (0, 0)),
        ],
        out_specs=[column, column, pl.BlockSpec((1, rows, LANES), lambda p: (p, 0, 0))],
        out_shape=[
            jax.ShapeDtypeStruct((rows, pairs * LANES), bf16),
            jax.ShapeDtypeStruct((rows, pairs * LANES), bf16),
            jax.ShapeDtypeStruct((pairs, rows, LANES), f32),
        ],
        scratch_shapes=[pltpu.VMEM((n_keys, LANES), bf16), pltpu.VMEM((n_keys, LANES), bf16)],
        compiler_params=pltpu.CompilerParams(
            dimension_semantics=("arbitrary",), vmem_limit_bytes=VMEM_LIMIT
        ),
        name="attend",
    )(kvq, kv, cosine, sine, places, key_places)


def attend_back_kernel(
    per_head, q_ref, kv_ref, lse_ref, grad_ref, cos_ref, sin_ref, place_ref, key_place_ref,
    dq_ref, dkv_ref, key_ref, value_ref, dk_acc, dv_acc,
):
    rows = q_ref.shape[0]
    half_rows, n_keys = rows // 2, kv_ref.shape[0]
    step = pl.program_id(0)
    load_keys(step, per_head, kv_ref, key_ref, value_ref)

    @pl.when(step % per_head == 0)
    def _():
        dk_acc[...] = jnp.zeros_like(dk_acc)
        dv_acc[...] = jnp.zeros_like(dv_acc)

    lane = lanes_of((half_rows, LANES))
    low = lane < HD
    for block in range(2):
        at, width = block * half_rows, (block + 1) * n_keys // 2
        chosen = q_ref[at : at + half_rows, :]
        upstream = grad_ref[at : at + half_rows, :]
        keys, values = key_ref[:width, :], value_ref[:width, :]
        causal = key_place_ref[:, :width] <= place_ref[at : at + half_rows, :]
        outs = []
        for part in range(2):
            mask = low if part == 0 else jnp.logical_not(low)
            one = jnp.where(mask, chosen, jnp.zeros_like(chosen))
            grad = jnp.where(mask, upstream, jnp.zeros_like(upstream))
            scores = SCALE * lax.dot_general(
                one, keys, (((1,), (1,)), ((), ())), preferred_element_type=f32
            )
            lse = lse_ref[0, at : at + half_rows, part * HD : part * HD + 1]
            probs = jnp.where(causal, jnp.exp(scores - lse), 0.0)
            prob_grad = lax.dot_general(
                grad, values, (((1,), (1,)), ((), ())), preferred_element_type=f32
            )
            inner = jnp.sum(probs * prob_grad, -1, keepdims=True)
            score_grad = (probs * (prob_grad - inner)).astype(bf16)
            outs.append(jnp.dot(score_grad, keys, preferred_element_type=f32) * SCALE)
            dk_acc[:width, :] += SCALE * lax.dot_general(
                score_grad, one, (((0,), (0,)), ((), ())), preferred_element_type=f32
            )
            dv_acc[:width, :] += lax.dot_general(
                probs.astype(bf16), grad, (((0,), (0,)), ((), ())), preferred_element_type=f32
            )
        total = jnp.where(low, outs[0], outs[1])
        dq_ref[at : at + half_rows, :] = (
            total * cos_ref[at : at + half_rows, :]
            - swap_halves(total, lane) * sin_ref[at : at + half_rows, :]
        ).astype(bf16)

    @pl.when(step % per_head == per_head - 1)
    def _():
        dk, dv = dk_acc[...], dv_acc[...]
        dk = dk + pltpu.roll(dk, HD, 1)
        dv = dv + pltpu.roll(dv, HD, 1)
        dkv_ref[...] = jnp.where(lanes_of(dk.shape) < HD, dk, dv).astype(bf16)


def attend_back(rope, kv, lse, grad, cosine, sine, places, key_places):
    rows, cols = rope.shape
    n_keys, kv_cols = kv.shape
    pairs, kv_heads = cols // LANES, kv_cols // LANES
    per_head = pairs // kv_heads
    whole = pl.BlockSpec((rows, LANES), lambda p: (0, 0))
    column = pl.BlockSpec((rows, LANES), lambda p: (0, p))
    keys = pl.BlockSpec((n_keys, LANES), lambda p: (0, p // per_head))
    return pl.pallas_call(
        functools.partial(attend_back_kernel, per_head),
        grid=(pairs,),
        in_specs=[
            column,
            keys,
            pl.BlockSpec((1, rows, LANES), lambda p: (p, 0, 0)),
            column,
            whole,
            whole,
            pl.BlockSpec((rows, 1), lambda p: (0, 0)),
            pl.BlockSpec((1, n_keys), lambda p: (0, 0)),
        ],
        out_specs=[column, keys],
        out_shape=[
            jax.ShapeDtypeStruct((rows, cols), bf16),
            jax.ShapeDtypeStruct((n_keys, kv_cols), bf16),
        ],
        scratch_shapes=[
            pltpu.VMEM((n_keys, LANES), bf16),
            pltpu.VMEM((n_keys, LANES), bf16),
            pltpu.VMEM((n_keys, LANES), f32),
            pltpu.VMEM((n_keys, LANES), f32),
        ],
        compiler_params=pltpu.CompilerParams(
            dimension_semantics=("arbitrary",), vmem_limit_bytes=VMEM_LIMIT
        ),
        name="attend_back",
    )(rope, kv, lse, grad, cosine, sine, places, key_places)


def ring(x, hop):
    size = lax.axis_size("mp")
    return lax.ppermute(x, "mp", [(k, (k + hop) % size) for k in range(size)])


def ring_gather(shard):
    return [shard] + [ring(shard, hop) for hop in range(1, lax.axis_size("mp"))]


def ring_scatter(pieces):
    total = pieces[0].astype(f32)
    for hop in range(1, len(pieces)):
        total = total + ring(pieces[hop], -hop).astype(f32)
    return total


def tie(values, filler):
    return lax.optimization_barrier((values, filler))


def line_gather(shard, fillers=()):
    size = lax.axis_size("mp")
    me = lax.axis_index("mp")
    fillers = list(fillers)
    ups, downs = [shard], [shard]
    for step in range(1, size):
        up = lax.ppermute(ups[-1], "mp", [(k, k + 1) for k in range(step - 1, size - 1)])
        down = lax.ppermute(downs[-1], "mp", [(k + 1, k) for k in range(size - step)])
        if step <= len(fillers):
            (up, down), fillers[step - 1] = tie((up, down), fillers[step - 1])
        ups.append(up)
        downs.append(down)
    pieces = [shard] + [
        jnp.where(me >= hop, ups[hop], downs[size - hop]) for hop in range(1, size)
    ]
    return jnp.concatenate(pieces), fillers


def line_scatter(parts, fillers=()):
    size = lax.axis_size("mp")
    parts = parts.reshape((size, -1) + parts.shape[1:])
    fillers = list(fillers)
    up, down = None, None
    for step in range(1, size):
        mine_up, mine_down = parts[step], parts[size - step]
        if step > 1:
            mine_up, mine_down = mine_up + up, mine_down + down
        up = lax.ppermute(mine_up, "mp", [(k, k + 1) for k in range(min(step, size - 1))])
        down = lax.ppermute(
            mine_down, "mp", [(k + 1, k) for k in range(max(size - 1 - step, 0), size - 1)]
        )
        if step <= len(fillers):
            (up, down), fillers[step - 1] = tie((up, down), fillers[step - 1])
    return parts[0].astype(f32) + up.astype(f32) + down.astype(f32), fillers


def adamw(weight, grad, mean_old, square_old, factor, rate, decay):
    clipped = grad.astype(f32) * factor
    mean_new = BETA_ONE * mean_old + (1 - BETA_ONE) * clipped
    square_new = BETA_TWO * square_old + (1 - BETA_TWO) * clipped * clipped
    ratio = (
        mean_new / (1 - BETA_ONE**STEP) / (jnp.sqrt(square_new / (1 - BETA_TWO**STEP)) + ADAM_EPS)
    )
    return (weight - rate * (ratio + decay * weight), mean_new, square_new)


def dot(a, b, dims=((1,), (0,)), out=f32):
    return lax.dot_general(a, b, (dims, ((), ())), preferred_element_type=f32).astype(out)


def body(
    tokens,
    targets,
    select,
    bucket,
    embed_table,
    query_weight,
    keyvalue_weight,
    output_weight,
    gateup_weight,
    down_weight,
    head_weight,
    norm_gains,
    embed_mean,
    query_mean,
    keyvalue_mean,
    output_mean,
    gateup_mean,
    down_mean,
    head_mean,
    gains_mean,
    embed_square,
    query_square,
    keyvalue_square,
    output_square,
    gateup_square,
    down_square,
    head_square,
    gains_square,
):
    n_dp, n_mp = lax.axis_size("dp"), lax.axis_size("mp")
    group = lax.axis_index("mp")
    rows = tokens.shape[0]
    home = rows // n_mp
    strip = home // 2
    table_rows, table_cols = embed_table.shape
    vocab_start = group * table_rows
    kv_cols = keyvalue_weight.shape[1]
    q_cols = query_weight.shape[1]
    others = (group - jnp.arange(n_mp)) % n_mp

    def by_piece(x):
        strips = x.reshape(x.shape[:-1] + (2 * n_mp, strip))
        first = strips[..., others, :]
        second = strips[..., 2 * n_mp - 1 - others, :]
        return jnp.concatenate([first, second], -1)

    def pair_heads(x):
        return x.reshape(-1, 2, KVH, HD).transpose(0, 2, 1, 3).reshape(-1, kv_cols)

    scales_int = select * bucket
    ids_scales = lax.all_gather(jnp.stack([tokens, scales_int]), "dp")
    gains_rows = lax.all_gather(norm_gains.astype(bf16), "dp", axis=1, tiled=True).astype(f32)

    def ordered(pieces, axis):
        stacked = jnp.stack(pieces)
        return jnp.concatenate([stacked[(group - k) % n_mp] for k in range(n_mp)], axis)

    query_rows = ordered(ring_gather(query_weight.astype(bf16)), 1)
    kvq_own = jnp.concatenate([pair_heads(keyvalue_weight.astype(bf16)), query_rows], 1)
    kvq_full = lax.all_gather(kvq_own, "dp", axis=0, tiled=True)
    output_rows = ordered(ring_gather(output_weight.astype(bf16)), 0)
    output_full = lax.all_gather(output_rows, "dp", axis=1, tiled=True)
    gateup_full = lax.all_gather(gateup_weight.astype(bf16), "dp", axis=1, tiled=True)
    down_full = lax.all_gather(down_weight.astype(bf16), "dp", axis=1, tiled=True)
    head_full = lax.all_gather(head_weight.astype(bf16), "dp", axis=0, tiled=True)

    positions = by_piece(jnp.arange(rows))
    cosine, sine = rotary_tables(positions[0])
    key_places = jnp.concatenate([positions[:, :strip].reshape(-1), positions[:, strip:].reshape(-1)])
    places, key_places = positions[0][:, None], key_places[None, :]

    weight_total = jnp.sum(ids_scales[:, 1]).astype(f32)
    ids_local = by_piece(ids_scales[:, 0]).transpose(1, 0, 2).reshape(-1) - vocab_start
    inside = (ids_local >= 0) & (ids_local < table_rows)
    looked = embed_table[jnp.clip(ids_local, 0, table_rows - 1)]
    looked = jnp.where(inside[:, None], looked, 0.0).astype(bf16)
    looked = line_scatter(looked)[0].astype(bf16)
    looked = lax.all_to_all(looked.reshape(n_dp, home, table_cols), "dp", 0, 0)
    start_rows = looked.transpose(1, 0, 2).reshape(home, -1).astype(f32)

    first_in = normed(start_rows, gains_rows[0]).astype(bf16)
    kvq = dot(first_in, kvq_full)
    kv_own = turn_keys(kvq, cosine, sine, 1.0, KVH)
    kv_pieces = ring_gather(kv_own)
    kv = jnp.concatenate([p[:strip] for p in kv_pieces] + [p[strip:] for p in kv_pieces])
    mixed, rope, lse = attend(kvq, kv, cosine, sine, places, key_places)
    middle_rows = start_rows + dot(mixed, output_full)

    second_in, _ = line_gather(normed(middle_rows, gains_rows[1]).astype(bf16))
    gate = dot(second_in, gateup_full[0])
    upper = dot(second_in, gateup_full[1])
    active = (jax.nn.silu(gate) * upper).astype(bf16)
    final_rows = middle_rows + line_scatter(dot(active, down_full, out=bf16))[0]

    final_in, _ = line_gather(normed(final_rows, gains_rows[2]).astype(bf16))
    head_cols = head_full.shape[1]
    goals = by_piece(targets).reshape(-1) - group * head_cols
    scales = by_piece(scales_int).reshape(-1).astype(f32)
    logits = dot(final_in, head_full)
    hits = jnp.arange(head_cols)[None, :] == goals[:, None]
    local_top = jnp.max(logits, -1)
    stats = jnp.stack(
        [
            local_top,
            jnp.sum(jnp.exp(logits - local_top[:, None]), -1),
            jnp.sum(jnp.where(hits, logits, 0.0), -1),
        ]
    ).reshape(3, n_mp, home)
    stats = lax.all_gather(stats[:, others], "mp")[:, :, others].reshape(n_mp, 3, rows)
    top = jnp.max(stats[:, 0], 0)
    expsum = jnp.sum(stats[:, 1] * jnp.exp(stats[:, 0] - top[None]), 0)
    logsum_all = top + jnp.log(expsum)
    picked = jnp.sum(stats[:, 2], 0)
    loss_part = jnp.sum(scales * (logsum_all - picked)) / n_mp
    coef = scales * (1.0 / weight_total)
    logit_grad = (
        (jnp.exp(logits - logsum_all[:, None]) - hits.astype(f32)) * coef[:, None]
    ).astype(bf16)

    def reduce_to(grad, axis):
        return lax.psum_scatter(grad, "dp", scatter_dimension=axis, tiled=True)

    final_partial = dot(logit_grad, head_full, ((1,), (1,)), bf16)
    final_grad, (head_grad,) = line_scatter(
        final_partial, [dot(final_in, logit_grad, ((0,), (0,)), bf16)]
    )
    head_part = reduce_to(head_grad, 0)
    residual, final_gain = norm_back(final_rows, gains_rows[2], final_grad)

    branch, _ = line_gather(residual.astype(bf16))
    sigmoid = jax.nn.sigmoid(gate)
    silu_gate = gate * sigmoid
    active_grad = dot(branch, down_full, ((1,), (1,)))
    gate_grad = (active_grad * upper * sigmoid * (1.0 + gate * (1.0 - sigmoid))).astype(bf16)
    upper_grad = (active_grad * silu_gate).astype(bf16)
    second_partial = (
        dot(gate_grad, gateup_full[0], ((1,), (1,)))
        + dot(upper_grad, gateup_full[1], ((1,), (1,)))
    ).astype(bf16)
    second_grad, (down_grad, gate_w, upper_w) = line_scatter(
        second_partial,
        [
            dot(active, branch, ((0,), (0,)), bf16),
            dot(second_in, gate_grad, ((0,), (0,)), bf16),
            dot(second_in, upper_grad, ((0,), (0,)), bf16),
        ],
    )
    down_part = reduce_to(down_grad, 1)
    gateup_part = reduce_to(jnp.stack([gate_w, upper_w]), 1)
    middle_extra, middle_gain = norm_back(middle_rows, gains_rows[1], second_grad)
    residual = residual + middle_extra

    branch = residual.astype(bf16)
    mixed_grad = dot(branch, output_full, ((1,), (1,)), bf16)
    query_pre, kv_grad = attend_back(rope, kv, lse, mixed_grad, cosine, sine, places, key_places)
    kv_halves = kv_grad.reshape(2, n_mp, strip, kv_cols)
    kv_grad = ring_scatter([jnp.concatenate([kv_halves[0, i], kv_halves[1, i]]) for i in range(n_mp)])
    kv_grad, output_grad = tie(kv_grad, dot(mixed, branch, ((0,), (0,)), bf16))
    pair_grad = turn_keys(kv_grad, cosine, sine, -1.0, KVH)
    kvq_grad = jnp.concatenate([pair_grad, query_pre], 1)
    first_grad = dot(kvq_grad, kvq_full, ((1,), (1,)))
    start_extra, start_gain = norm_back(start_rows, gains_rows[0], first_grad)
    start_grad = (residual + start_extra).astype(bf16)
    gains_grad = jnp.stack([start_gain, middle_gain, final_gain], 1).astype(bf16)
    kvq_w = jnp.concatenate([dot(first_in, kvq_grad, ((0,), (0,)), bf16), gains_grad], 1)
    start_grad, kvq_w = tie(start_grad, kvq_w)

    kvq_w = reduce_to(kvq_w, 0)
    output_w = reduce_to(output_grad, 1)

    def piece_of(x, hop, axis, length):
        return lax.dynamic_slice_in_dim(x, (group - hop) % n_mp * length, length, axis)

    query_part = ring_scatter(
        [piece_of(kvq_w[:, kv_cols : kv_cols + q_cols * n_mp], i, 1, q_cols) for i in range(n_mp)]
    )
    output_part = ring_scatter(
        [piece_of(output_w, i, 0, output_weight.shape[0]) for i in range(n_mp)]
    )
    shared = jnp.concatenate([kvq_w[:, :kv_cols], kvq_w[:, kv_cols + q_cols * n_mp :]], 1)
    shared = ring_scatter([shared] * n_mp)
    gains_part = shared[:, kv_cols:].T
    keyvalue_part = (
        shared[:, :kv_cols].reshape(-1, KVH, 2, HD).transpose(0, 2, 1, 3).reshape(-1, kv_cols)
    )

    moved = start_grad.reshape(home, n_dp, table_cols).transpose(1, 0, 2)
    moved = lax.all_to_all(moved, "dp", 0, 0)
    moved, _ = line_gather(moved.reshape(n_dp * home, table_cols))
    onehot = (ids_local[None, :] == jnp.arange(table_rows)[:, None]).astype(bf16)
    embed_part = dot(onehot, moved)

    leading = (group == 0).astype(f32)

    def square(piece):
        piece = piece.astype(f32)
        return jnp.sum(piece * piece)

    squared = sum(
        square(piece)
        for piece in (embed_part, query_part, output_part, gateup_part, down_part, head_part)
    )
    squared = squared + leading * (square(keyvalue_part) + square(gains_part))
    squared, loss_sum = lax.psum((squared, loss_part), ("dp", "mp"))
    grad_norm = jnp.sqrt(squared)
    factor = jnp.minimum(1.0, CLIP / (grad_norm + 1e-06))
    outs = [loss_sum, weight_total, grad_norm]
    for number, (weight, grad, mean_old, square_old) in enumerate(
        (
            (embed_table, embed_part, embed_mean, embed_square),
            (query_weight, query_part, query_mean, query_square),
            (keyvalue_weight, keyvalue_part, keyvalue_mean, keyvalue_square),
            (output_weight, output_part, output_mean, output_square),
            (gateup_weight, gateup_part, gateup_mean, gateup_square),
            (down_weight, down_part, down_mean, down_square),
            (head_weight, head_part, head_mean, head_square),
            (norm_gains, gains_part, gains_mean, gains_square),
        )
    ):
        new, mean_new, square_new = adamw(
            weight, grad, mean_old, square_old, factor, RATES[number], DECAYS[number]
        )
        outs += [new, embed_part * factor if number == 0 else mean_new, square_new]
    return tuple(outs)


def solution(mesh):
    weights = (
        P("mp", "dp"),
        P("dp", "mp"),
        P("dp", None),
        P("mp", "dp"),
        P(None, "dp", "mp"),
        P("mp", "dp"),
        P("dp", "mp"),
        P(None, "dp"),
    )
    in_specs = (P("dp"),) * 4 + weights * 3
    out_specs = (P(),) * 3 + tuple(spec for spec in weights for _ in range(3))
    return jax.shard_map(body, mesh=mesh, in_specs=in_specs, out_specs=out_specs, check_vma=False)
```

```python
import functools

import jax
import jax.numpy as jnp
from jax import lax
from jax.experimental import pallas as pl
from jax.experimental.pallas import tpu as pltpu
from jax.sharding import PartitionSpec as P

HD = 64
KVH = 4
LEN = 1024
STEP = 5

EPS = 1e-05
SCALE = 0.125
CLIP = 0.01
BETA_ONE = 0.9
BETA_TWO = 0.95
ADAM_EPS = 1e-08
RATES = (0.9, 0.01, 0.01, 0.06, 0.01, 0.01, 0.08, 0.9)
DECAYS = (0.1, 0.1, 0.1, 0.1, 0.1, 0.1, 0.1, 0.0)

LANES = 128
VMEM_LIMIT = 56 * 1024 * 1024

f32 = jnp.float32
bf16 = jnp.bfloat16


def normed(hidden, gain):
    return hidden * lax.rsqrt(jnp.mean(hidden * hidden, axis=-1, keepdims=True) + EPS) * gain


def norm_back(hidden, gain, upstream):
    _, pullback = jax.vjp(normed, hidden, gain)
    return pullback(upstream)


def rotary_tables(places):
    freqs = 10000.0 ** (-(2 * jnp.arange(HD // 2)).astype(f32) / HD)
    angles = (places % LEN).astype(f32)[:, None] * freqs[None, :]
    cosine = jnp.cos(angles)
    sine = jnp.sin(angles)
    return (
        jnp.concatenate([cosine] * 4, -1),
        jnp.concatenate([-sine, sine, -sine, sine], -1),
    )


def swap_halves(x, lane):
    half = HD // 2
    return jnp.where(
        lane % HD < half, pltpu.roll(x, LANES - half, 1), pltpu.roll(x, half, 1)
    )


def lanes_of(shape):
    return lax.broadcasted_iota(jnp.int32, shape, 1)


def turn_kernel(sign, kv_ref, cos_ref, sin_ref, out_ref):
    rows = kv_ref.shape[0]
    lane = lanes_of((rows, LANES))
    x = kv_ref[...]
    turned = x * cos_ref[...] + sign * swap_halves(x, lane) * sin_ref[...]
    out_ref[...] = jnp.where(lane < HD, turned, x).astype(bf16)


def turn_keys(kv, cosine, sine, sign, n_heads):
    rows = kv.shape[0]
    column = pl.BlockSpec((rows, LANES), lambda p: (0, p))
    whole = pl.BlockSpec((rows, LANES), lambda p: (0, 0))
    return pl.pallas_call(
        functools.partial(turn_kernel, sign),
        grid=(n_heads,),
        in_specs=[column, whole, whole],
        out_specs=column,
        out_shape=jax.ShapeDtypeStruct((rows, n_heads * LANES), bf16),
        name="turn_keys",
    )(kv, cosine, sine)


def load_keys(step, per_head, kv_ref, key_ref, value_ref):
    @pl.when(step % per_head == 0)
    def _():
        pair = kv_ref[...].astype(f32)
        other = pltpu.roll(pair, HD, 1)
        lane = lanes_of(pair.shape)
        key_ref[...] = jnp.where(lane < HD, pair, other).astype(bf16)
        value_ref[...] = jnp.where(lane < HD, other, pair).astype(bf16)


def both_heads(pair, low):
    zero = jnp.zeros_like(pair)
    return jnp.concatenate([jnp.where(low, pair, zero), jnp.where(low, zero, pair)])


def contract(a, b, dims):
    return lax.dot_general(a, b, (((dims[0],), (dims[1],)), ((), ())), preferred_element_type=f32)


def attend_kernel(
    per_head, q_ref, kv_ref, cos_ref, sin_ref, place_ref, key_place_ref,
    mixed_ref, rope_ref, lse_ref, key_ref, value_ref,
):
    rows = q_ref.shape[0]
    half_rows, n_keys = rows // 2, kv_ref.shape[0]
    load_keys(pl.program_id(0), per_head, kv_ref, key_ref, value_ref)
    q = q_ref[...]
    rope_ref[...] = (q * cos_ref[...] + swap_halves(q, lanes_of(q.shape)) * sin_ref[...]).astype(bf16)
    low = lanes_of((half_rows, LANES)) < HD
    for block in range(2):
        at, width = block * half_rows, (block + 1) * n_keys // 2
        chosen = both_heads(rope_ref[at : at + half_rows, :], low)
        scores = SCALE * contract(key_ref[:width, :], chosen, (1, 1))
        causal = key_place_ref[:width, :] <= place_ref[block : block + 1, :]
        scores = jnp.where(causal, scores, -1e30)
        peak = jnp.max(scores, 0, keepdims=True)
        expo = jnp.exp(scores - peak)
        total = jnp.sum(expo, 0, keepdims=True)
        probs = (expo * (1.0 / total)).astype(bf16)
        out = contract(probs, value_ref[:width, :], (0, 0))
        mixed_ref[at : at + half_rows, :] = jnp.where(
            low, out[:half_rows], out[half_rows:]
        ).astype(bf16)
        lse_ref[0, block : block + 1, :] = peak + jnp.log(total)


def attend(q, kv, cosine, sine, places, key_places):
    rows, cols = q.shape
    n_keys, kv_cols = kv.shape
    pairs, kv_heads = cols // LANES, kv_cols // LANES
    per_head = pairs // kv_heads
    whole = pl.BlockSpec((rows, LANES), lambda p: (0, 0))
    column = pl.BlockSpec((rows, LANES), lambda p: (0, p))
    return pl.pallas_call(
        functools.partial(attend_kernel, per_head),
        grid=(pairs,),
        in_specs=[
            column,
            pl.BlockSpec((n_keys, LANES), lambda p: (0, p // per_head)),
            whole,
            whole,
            pl.BlockSpec((2, rows), lambda p: (0, 0)),
            pl.BlockSpec((n_keys, 1), lambda p: (0, 0)),
        ],
        out_specs=[column, column, pl.BlockSpec((1, 2, rows), lambda p: (p, 0, 0))],
        out_shape=[
            jax.ShapeDtypeStruct((rows, cols), bf16),
            jax.ShapeDtypeStruct((rows, cols), bf16),
            jax.ShapeDtypeStruct((pairs, 2, rows), f32),
        ],
        scratch_shapes=[pltpu.VMEM((n_keys, LANES), bf16), pltpu.VMEM((n_keys, LANES), bf16)],
        compiler_params=pltpu.CompilerParams(
            dimension_semantics=("arbitrary",), vmem_limit_bytes=VMEM_LIMIT
        ),
        name="attend",
    )(q, kv, cosine, sine, places, key_places)


def attend_back_kernel(
    per_head, q_ref, kv_ref, lse_ref, grad_ref, cos_ref, sin_ref, place_ref, key_place_ref,
    dq_ref, dkv_ref, key_ref, value_ref, dk_acc, dv_acc,
):
    rows = q_ref.shape[0]
    half_rows, n_keys = rows // 2, kv_ref.shape[0]
    step = pl.program_id(0)
    load_keys(step, per_head, kv_ref, key_ref, value_ref)

    @pl.when(step % per_head == 0)
    def _():
        dk_acc[...] = jnp.zeros_like(dk_acc)
        dv_acc[...] = jnp.zeros_like(dv_acc)

    lane = lanes_of((half_rows, LANES))
    low = lane < HD
    for block in range(2):
        at, width = block * half_rows, (block + 1) * n_keys // 2
        chosen = both_heads(q_ref[at : at + half_rows, :], low)
        grad = both_heads(grad_ref[at : at + half_rows, :], low)
        keys, values = key_ref[:width, :], value_ref[:width, :]
        scores = SCALE * contract(keys, chosen, (1, 1))
        causal = key_place_ref[:width, :] <= place_ref[block : block + 1, :]
        probs = jnp.where(causal, jnp.exp(scores - lse_ref[0, block : block + 1, :]), 0.0)
        prob_grad = contract(values, grad, (1, 1))
        inner = jnp.sum(probs * prob_grad, 0, keepdims=True)
        score_grad = (probs * (prob_grad - inner)).astype(bf16)
        dk_acc[:width, :] += SCALE * contract(score_grad, chosen, (1, 0))
        dv_acc[:width, :] += contract(probs.astype(bf16), grad, (1, 0))
        out = SCALE * contract(score_grad, keys, (0, 0))
        total = jnp.where(low, out[:half_rows], out[half_rows:])
        dq_ref[at : at + half_rows, :] = (
            total * cos_ref[at : at + half_rows, :]
            - swap_halves(total, lane) * sin_ref[at : at + half_rows, :]
        ).astype(bf16)

    @pl.when(step % per_head == per_head - 1)
    def _():
        dk, dv = dk_acc[...], dv_acc[...]
        dk = dk + pltpu.roll(dk, HD, 1)
        dv = dv + pltpu.roll(dv, HD, 1)
        dkv_ref[...] = jnp.where(lanes_of(dk.shape) < HD, dk, dv).astype(bf16)


def attend_back(rope, kv, lse, grad, cosine, sine, places, key_places):
    rows, cols = rope.shape
    n_keys, kv_cols = kv.shape
    pairs, kv_heads = cols // LANES, kv_cols // LANES
    per_head = pairs // kv_heads
    whole = pl.BlockSpec((rows, LANES), lambda p: (0, 0))
    column = pl.BlockSpec((rows, LANES), lambda p: (0, p))
    keys = pl.BlockSpec((n_keys, LANES), lambda p: (0, p // per_head))
    return pl.pallas_call(
        functools.partial(attend_back_kernel, per_head),
        grid=(pairs,),
        in_specs=[
            column,
            keys,
            pl.BlockSpec((1, 2, rows), lambda p: (p, 0, 0)),
            column,
            whole,
            whole,
            pl.BlockSpec((2, rows), lambda p: (0, 0)),
            pl.BlockSpec((n_keys, 1), lambda p: (0, 0)),
        ],
        out_specs=[column, keys],
        out_shape=[
            jax.ShapeDtypeStruct((rows, cols), bf16),
            jax.ShapeDtypeStruct((n_keys, kv_cols), bf16),
        ],
        scratch_shapes=[
            pltpu.VMEM((n_keys, LANES), bf16),
            pltpu.VMEM((n_keys, LANES), bf16),
            pltpu.VMEM((n_keys, LANES), f32),
            pltpu.VMEM((n_keys, LANES), f32),
        ],
        compiler_params=pltpu.CompilerParams(
            dimension_semantics=("arbitrary",), vmem_limit_bytes=VMEM_LIMIT
        ),
        name="attend_back",
    )(rope, kv, lse, grad, cosine, sine, places, key_places)


def ring(x, hop):
    size = lax.axis_size("mp")
    return lax.ppermute(x, "mp", [(k, (k + hop) % size) for k in range(size)])


def ring_gather(shard):
    return [shard] + [ring(shard, hop) for hop in range(1, lax.axis_size("mp"))]


def ring_scatter(pieces):
    total = pieces[0].astype(f32)
    for hop in range(1, len(pieces)):
        total = total + ring(pieces[hop], -hop).astype(f32)
    return total


def tie(values, filler):
    return lax.optimization_barrier((values, filler))


def piece_order():
    size = lax.axis_size("mp")
    order = []
    for step in range(1, size // 2 + 1):
        order += [step, size - step] if 2 * step < size else [step]
    return order + [0]


def line_gather(shard):
    size = lax.axis_size("mp")
    me = lax.axis_index("mp")
    ups, downs = [shard], [shard]
    for step in range(1, size):
        ups.append(lax.ppermute(ups[-1], "mp", [(k, k + 1) for k in range(step - 1, size - 1)]))
        downs.append(lax.ppermute(downs[-1], "mp", [(k + 1, k) for k in range(size - step)]))
    pieces = [shard] + [
        jnp.where(me >= hop, ups[hop], downs[size - hop]) for hop in range(1, size)
    ]
    return jnp.concatenate([pieces[i] for i in piece_order()])


def arrivals(shard):
    size = lax.axis_size("mp")
    me = lax.axis_index("mp")
    yield me, shard
    up, downs = shard, [shard]
    for step in range(1, size):
        up = lax.ppermute(up, "mp", [(k, k + 1) for k in range(step - 1, size - 1)])
        downs.append(lax.ppermute(downs[-1], "mp", [(k + 1, k) for k in range(size - step)]))
        piece = up
        for place in range(step):
            piece = jnp.where(me == place, downs[step - place], piece)
        yield jnp.where(me >= step, me - step, step), piece


def line_scatter(parts, fillers=()):
    size = lax.axis_size("mp")
    split = []
    for part in parts:
        split += list(part.reshape((size // len(parts), -1) + part.shape[1:]))
    piece = dict(zip(piece_order(), split))
    fillers = list(fillers)
    up, down = None, None
    for step in range(1, size):
        mine_up, mine_down = piece[step], piece[size - step]
        if step > 1:
            mine_up, mine_down = mine_up + up, mine_down + down
        up = lax.ppermute(mine_up, "mp", [(k, k + 1) for k in range(min(step, size - 1))])
        down = lax.ppermute(
            mine_down, "mp", [(k + 1, k) for k in range(max(size - 1 - step, 0), size - 1)]
        )
        if step <= len(fillers):
            (up, down), fillers[step - 1] = tie((up, down), fillers[step - 1])
        if step == 2:
            (up, down), piece[0] = tie((up, down), piece[0])
    return piece[0].astype(f32) + up.astype(f32) + down.astype(f32), fillers


def halves(x):
    n = x.shape[0] // 2
    return [x[:n], x[n:]]


def adamw(weight, grad, mean_old, square_old, factor, rate, decay):
    clipped = grad.astype(f32) * factor
    mean_new = BETA_ONE * mean_old + (1 - BETA_ONE) * clipped
    square_new = BETA_TWO * square_old + (1 - BETA_TWO) * clipped * clipped
    ratio = (
        mean_new / (1 - BETA_ONE**STEP) / (jnp.sqrt(square_new / (1 - BETA_TWO**STEP)) + ADAM_EPS)
    )
    return (weight - rate * (ratio + decay * weight), mean_new, square_new)


def dot(a, b, dims=((1,), (0,)), out=f32):
    return lax.dot_general(a, b, (dims, ((), ())), preferred_element_type=f32).astype(out)


def body(
    tokens,
    targets,
    select,
    bucket,
    embed_table,
    query_weight,
    keyvalue_weight,
    output_weight,
    gateup_weight,
    down_weight,
    head_weight,
    norm_gains,
    embed_mean,
    query_mean,
    keyvalue_mean,
    output_mean,
    gateup_mean,
    down_mean,
    head_mean,
    gains_mean,
    embed_square,
    query_square,
    keyvalue_square,
    output_square,
    gateup_square,
    down_square,
    head_square,
    gains_square,
):
    n_dp, n_mp = lax.axis_size("dp"), lax.axis_size("mp")
    group = lax.axis_index("mp")
    rows = tokens.shape[0]
    home = rows // n_mp
    strip = home // 2
    table_rows, table_cols = embed_table.shape
    vocab_start = group * table_rows
    kv_cols = keyvalue_weight.shape[1]
    q_cols = query_weight.shape[1]
    ring_order = (group - jnp.arange(n_mp)) % n_mp
    line_order = (group - jnp.array(piece_order())) % n_mp

    def by_piece(x, order):
        strips = x.reshape(x.shape[:-1] + (2 * n_mp, strip))
        first = strips[..., order, :]
        second = strips[..., 2 * n_mp - 1 - order, :]
        return jnp.concatenate([first, second], -1)

    def pair_heads(x):
        return x.reshape(-1, 2, KVH, HD).transpose(0, 2, 1, 3).reshape(-1, kv_cols)

    scales_int = select * bucket
    meta = jnp.concatenate(
        [tokens.astype(f32), scales_int.astype(f32), norm_gains.astype(bf16).astype(f32).reshape(-1)]
    )
    meta = lax.all_gather(meta, "dp")
    ids = meta[:, :rows].astype(jnp.int32)
    gains_rows = meta[:, 2 * rows :].reshape(n_dp, 3, -1).transpose(1, 0, 2).reshape(3, -1)

    def ordered(pieces, axis):
        stacked = jnp.stack(pieces)
        return jnp.concatenate([stacked[(group - k) % n_mp] for k in range(n_mp)], axis)

    weight_total = jnp.sum(meta[:, rows : 2 * rows])
    ids_local = by_piece(ids, line_order).transpose(1, 0, 2) - vocab_start

    def look_up(piece_ids):
        inside = (piece_ids >= 0) & (piece_ids < table_rows)
        found = embed_table[jnp.clip(piece_ids, 0, table_rows - 1)]
        return jnp.where(inside[:, None], found, 0.0).astype(bf16)

    looked = [look_up(ids_local[i].reshape(-1)) for i in range(n_mp)]
    ids_local = ids_local.reshape(-1)

    query_pieces = ring_gather(query_weight.astype(bf16))
    output_pieces = ring_gather(output_weight.astype(bf16))
    looked[: n_mp // 2], (query_pieces, output_pieces) = tie(
        looked[: n_mp // 2], (query_pieces, output_pieces)
    )
    kvq_own = jnp.concatenate(
        [pair_heads(keyvalue_weight.astype(bf16)), ordered(query_pieces, 1)], 1
    )
    kvq_full = lax.all_gather(kvq_own, "dp", axis=0, tiled=True)
    looked, (gateup_own, down_own, head_own) = line_scatter(
        looked,
        [
            gateup_weight.astype(bf16).transpose(1, 0, 2).reshape(table_cols, -1),
            down_weight.astype(bf16),
            head_weight.astype(bf16),
        ],
    )
    output_own = ordered(output_pieces, 0)
    gateup_full = lax.all_gather(gateup_own, "dp", axis=0, tiled=True)
    output_full = lax.all_gather(output_own, "dp", axis=1, tiled=True)
    down_full = lax.all_gather(down_own, "dp", axis=1, tiled=True)
    head_full = lax.all_gather(head_own, "dp", axis=0, tiled=True)

    positions = by_piece(jnp.arange(rows), ring_order)
    cosine, sine = rotary_tables(positions[0])
    key_places = jnp.concatenate([positions[:, :strip].reshape(-1), positions[:, strip:].reshape(-1)])
    places, key_places = jnp.tile(positions[0].reshape(2, strip), (1, 2)), key_places[:, None]

    looked = looked.astype(bf16)
    looked = lax.all_to_all(looked.reshape(n_dp, home, table_cols), "dp", 0, 0)
    start_rows = looked.transpose(1, 0, 2).reshape(home, -1).astype(f32)

    first_in = normed(start_rows, gains_rows[0]).astype(bf16)
    kv_own = turn_keys(dot(first_in, kvq_full[:, :kv_cols]), cosine, sine, 1.0, KVH)
    queries = dot(first_in, kvq_full[:, kv_cols:])
    kv_pieces = ring_gather(kv_own)
    kv = jnp.concatenate([p[:strip] for p in kv_pieces] + [p[strip:] for p in kv_pieces])
    mixed, rope, lse = attend(queries, kv, cosine, sine, places, key_places)
    middle_rows = start_rows + dot(mixed, output_full)

    second_in = line_gather(normed(middle_rows, gains_rows[1]).astype(bf16))
    gate_upper = dot(second_in, gateup_full)
    half = gate_upper.shape[1] // 2
    gate, upper = gate_upper[:, :half], gate_upper[:, half:]
    active = (jax.nn.silu(gate) * upper).astype(bf16)
    final_rows = middle_rows + line_scatter([dot(a, down_full, out=bf16) for a in halves(active)])[0]

    final_in = line_gather(normed(final_rows, gains_rows[2]).astype(bf16))
    head_cols = head_full.shape[1]
    goals = by_piece(targets, line_order).reshape(-1) - group * head_cols
    scales = by_piece(scales_int, line_order).reshape(-1).astype(f32)
    logits = dot(final_in, head_full)
    hits = jnp.arange(head_cols)[None, :] == goals[:, None]
    local_top = jnp.max(logits, -1)
    stats = jnp.stack(
        [
            local_top,
            jnp.sum(jnp.exp(logits - local_top[:, None]), -1),
            jnp.sum(jnp.where(hits, logits, 0.0), -1),
        ]
    ).reshape(3, n_mp, home)
    back = [piece_order().index(i) for i in range(n_mp)]
    stats = stats[:, jnp.array(back)[ring_order]]
    stats = jnp.stack(ring_gather(stats))[:, :, line_order].reshape(n_mp, 3, rows)
    top = jnp.max(stats[:, 0], 0)
    expsum = jnp.sum(stats[:, 1] * jnp.exp(stats[:, 0] - top[None]), 0)
    logsum_all = top + jnp.log(expsum)
    picked = jnp.sum(stats[:, 2], 0)
    loss_part = jnp.sum(scales * (logsum_all - picked)) / n_mp
    coef = scales * (1.0 / weight_total)
    logit_grad = (
        (jnp.exp(logits - logsum_all[:, None]) - hits.astype(f32)) * coef[:, None]
    ).astype(bf16)

    def reduce_to(grad, axis):
        return lax.psum_scatter(grad, "dp", scatter_dimension=axis, tiled=True)

    final_partial = [dot(logit_grad, head_full, ((1,), (1,)), bf16)]
    final_grad, (head_grad,) = line_scatter(
        final_partial, [dot(final_in, logit_grad, ((0,), (0,)), bf16)]
    )
    head_part = reduce_to(head_grad, 0)
    residual, final_gain = norm_back(final_rows, gains_rows[2], final_grad)

    branch = line_gather(residual.astype(bf16))
    sigmoid = jax.nn.sigmoid(gate)
    silu_gate = gate * sigmoid
    active_grad = dot(branch, down_full, ((1,), (1,)))
    gate_grad = (active_grad * upper * sigmoid * (1.0 + gate * (1.0 - sigmoid))).astype(bf16)
    upper_grad = (active_grad * silu_gate).astype(bf16)
    gateup_grad = jnp.concatenate([gate_grad, upper_grad], 1)
    second_partial = [dot(g, gateup_full, ((1,), (1,)), bf16) for g in halves(gateup_grad)]
    second_grad, (down_grad, gateup_w) = line_scatter(
        second_partial,
        [
            dot(active, branch, ((0,), (0,)), bf16),
            dot(second_in, gateup_grad, ((0,), (0,)), bf16),
        ],
    )
    (down_grad, gateup_w), head_part = tie((down_grad, gateup_w), head_part)
    down_part = reduce_to(down_grad, 1)
    gateup_part = reduce_to(gateup_w, 0)
    middle_extra, middle_gain = norm_back(middle_rows, gains_rows[1], second_grad)
    residual = residual + middle_extra

    branch = residual.astype(bf16)
    branch, output_w = tie(branch, dot(mixed, branch, ((0,), (0,)), bf16))
    output_w, down_part = tie(output_w, down_part)
    output_w = reduce_to(output_w, 1)
    mixed_grad = dot(branch, output_full, ((1,), (1,)), bf16)
    query_pre, kv_grad = attend_back(rope, kv, lse, mixed_grad, cosine, sine, places, key_places)
    kv_halves = kv_grad.reshape(2, n_mp, strip, kv_cols)
    kv_grad = ring_scatter([jnp.concatenate([kv_halves[0, i], kv_halves[1, i]]) for i in range(n_mp)])
    pair_grad = turn_keys(kv_grad, cosine, sine, -1.0, KVH)
    kvq_grad = jnp.concatenate([pair_grad, query_pre], 1)
    kvq_grad, kvq_w = tie(kvq_grad, dot(first_in, kvq_grad, ((0,), (0,)), bf16))
    first_grad = dot(kvq_grad, kvq_full, ((1,), (1,)))
    start_extra, start_gain = norm_back(start_rows, gains_rows[0], first_grad)
    start_grad = (residual + start_extra).astype(bf16)
    gains_grad = jnp.stack([start_gain, middle_gain, final_gain]).astype(bf16)

    def piece_of(x, hop, axis, length):
        return lax.dynamic_slice_in_dim(x, (group - hop) % n_mp * length, length, axis)

    moved = jnp.concatenate([start_grad, gains_grad, jnp.zeros((13, start_grad.shape[1]), bf16)])
    moved = moved.reshape(-1, n_dp, table_cols).transpose(1, 0, 2)
    moved = lax.all_to_all(moved, "dp", 0, 0)
    kvq_w, (gateup_part, _) = tie(kvq_w, (gateup_part, moved[0, :16]))
    gateup_part = gateup_part.reshape(table_cols, 2, -1).transpose(1, 0, 2)
    gains_part = ring_scatter([jnp.sum(moved[:, home : home + 3].astype(f32), 0)] * n_mp)
    embed_part = None
    ids_home = by_piece(ids, jnp.arange(n_mp)).transpose(1, 0, 2).reshape(n_mp, -1) - vocab_start
    for device, shard in arrivals(moved[:, :home].reshape(n_dp * home, table_cols)):
        onehot = (ids_home[device][None, :] == jnp.arange(table_rows)[:, None]).astype(bf16)
        part = dot(onehot, shard)
        embed_part = part if embed_part is None else embed_part + part

    kvq_w = reduce_to(kvq_w, 0)
    output_w, embed_part = tie(output_w, embed_part)
    query_part = ring_scatter(
        [piece_of(kvq_w[:, kv_cols:], i, 1, q_cols) for i in range(n_mp)]
    )
    keyvalue_part = ring_scatter([kvq_w[:, :kv_cols]] * n_mp)
    keyvalue_part = keyvalue_part.reshape(-1, KVH, 2, HD).transpose(0, 2, 1, 3).reshape(-1, kv_cols)
    output_part = ring_scatter(
        [piece_of(output_w, i, 0, output_weight.shape[0]) for i in range(n_mp)]
    )

    leading = (group == 0).astype(f32)

    def square(piece):
        piece = piece.astype(f32)
        return jnp.sum(piece * piece)

    squared = sum(
        square(piece)
        for piece in (embed_part, query_part, output_part, gateup_part, down_part, head_part)
    )
    squared = squared + leading * (square(keyvalue_part) + square(gains_part))
    totals = jnp.stack([squared, loss_part])[:, None]
    totals = sum(ring_gather(totals))
    hop = 1
    while hop < n_dp:
        totals = totals + lax.ppermute(totals, "dp", [(k, k ^ hop) for k in range(n_dp)])
        hop *= 2
    grad_norm, loss_sum = jnp.sqrt(totals[0, 0]), totals[1, 0]
    factor = jnp.minimum(1.0, CLIP / (grad_norm + 1e-06))
    outs = [loss_sum, weight_total, grad_norm]
    for number, (weight, grad, mean_old, square_old) in enumerate(
        (
            (embed_table, embed_part, embed_mean, embed_square),
            (query_weight, query_part, query_mean, query_square),
            (keyvalue_weight, keyvalue_part, keyvalue_mean, keyvalue_square),
            (output_weight, output_part, output_mean, output_square),
            (gateup_weight, gateup_part, gateup_mean, gateup_square),
            (down_weight, down_part, down_mean, down_square),
            (head_weight, head_part, head_mean, head_square),
            (norm_gains, gains_part, gains_mean, gains_square),
        )
    ):
        new, mean_new, square_new = adamw(
            weight, grad, mean_old, square_old, factor, RATES[number], DECAYS[number]
        )
        outs += [new, embed_part * factor if number == 0 else mean_new, square_new]
    return tuple(outs)


def solution(mesh):
    weights = (
        P("mp", "dp"),
        P("dp", "mp"),
        P("dp", None),
        P("mp", "dp"),
        P(None, "dp", "mp"),
        P("mp", "dp"),
        P("dp", "mp"),
        P(None, "dp"),
    )
    in_specs = (P("dp"),) * 4 + weights * 3
    out_specs = (P(),) * 3 + tuple(spec for spec in weights for _ in range(3))
    return jax.shard_map(body, mesh=mesh, in_specs=in_specs, out_specs=out_specs, check_vma=False)
```

```python
import functools

import jax
import jax.numpy as jnp
from jax import lax
from jax.experimental import pallas as pl
from jax.experimental.pallas import tpu as pltpu
from jax.sharding import PartitionSpec as P

HD = 64
KVH = 4
LEN = 1024
STEP = 5

EPS = 1e-05
SCALE = 0.125
CLIP = 0.01
BETA_ONE = 0.9
BETA_TWO = 0.95
ADAM_EPS = 1e-08
RATES = (0.9, 0.01, 0.01, 0.06, 0.01, 0.01, 0.08, 0.9)
DECAYS = (0.1, 0.1, 0.1, 0.1, 0.1, 0.1, 0.1, 0.0)

LANES = 128
VMEM_LIMIT = 56 * 1024 * 1024

f32 = jnp.float32
bf16 = jnp.bfloat16


def normed(hidden, gain):
    return hidden * lax.rsqrt(jnp.mean(hidden * hidden, axis=-1, keepdims=True) + EPS) * gain


def norm_back(hidden, gain, upstream):
    _, pullback = jax.vjp(normed, hidden, gain)
    return pullback(upstream)


def rotary_tables(places):
    freqs = 10000.0 ** (-(2 * jnp.arange(HD // 2)).astype(f32) / HD)
    angles = (places % LEN).astype(f32)[:, None] * freqs[None, :]
    cosine = jnp.cos(angles)
    sine = jnp.sin(angles)
    return (
        jnp.concatenate([cosine] * 4, -1),
        jnp.concatenate([-sine, sine, -sine, sine], -1),
    )


def swap_halves(x, lane):
    half = HD // 2
    return jnp.where(
        lane % HD < half, pltpu.roll(x, LANES - half, 1), pltpu.roll(x, half, 1)
    )


def lanes_of(shape):
    return lax.broadcasted_iota(jnp.int32, shape, 1)


def turn_kernel(sign, kv_ref, cos_ref, sin_ref, out_ref):
    rows = kv_ref.shape[0]
    lane = lanes_of((rows, LANES))
    x = kv_ref[...]
    turned = x * cos_ref[...] + sign * swap_halves(x, lane) * sin_ref[...]
    out_ref[...] = jnp.where(lane < HD, turned, x).astype(bf16)


def turn_keys(kv, cosine, sine, sign, n_heads):
    rows = kv.shape[0]
    column = pl.BlockSpec((rows, LANES), lambda p: (0, p))
    whole = pl.BlockSpec((rows, LANES), lambda p: (0, 0))
    return pl.pallas_call(
        functools.partial(turn_kernel, sign),
        grid=(n_heads,),
        in_specs=[column, whole, whole],
        out_specs=column,
        out_shape=jax.ShapeDtypeStruct((rows, n_heads * LANES), bf16),
        name="turn_keys",
    )(kv, cosine, sine)


def load_keys(step, per_head, kv_ref, key_ref, value_ref, turned_ref, turn_key):
    @pl.when(step % per_head == 0)
    def _():
        pair = kv_ref[...].astype(f32)
        other = pltpu.roll(pair, HD, 1)
        lane = lanes_of(pair.shape)
        key = jnp.where(lane < HD, pair, other)
        value = jnp.where(lane < HD, other, pair)
        key_ref[...] = key.astype(bf16)
        if value_ref is not None:
            value_ref[...] = value.astype(bf16)
        turned_ref[...] = (key if turn_key else value).T.astype(bf16)


def both_heads(pair, low):
    zero = jnp.zeros_like(pair)
    return jnp.concatenate([jnp.where(low, pair, zero), jnp.where(low, zero, pair)])


def contract(a, b, dims):
    return lax.dot_general(a, b, (((dims[0],), (dims[1],)), ((), ())), preferred_element_type=f32)


def attend_kernel(
    per_head, q_ref, kv_ref, cos_ref, sin_ref, place_ref, key_place_ref,
    mixed_ref, rope_ref, lse_ref, key_ref, turned_ref,
):
    rows = q_ref.shape[0]
    half_rows, n_keys = rows // 2, kv_ref.shape[0]
    load_keys(pl.program_id(0), per_head, kv_ref, key_ref, None, turned_ref, False)
    q = q_ref[...]
    q = (q * cos_ref[...] + swap_halves(q, lanes_of(q.shape)) * sin_ref[...]).astype(bf16)
    rope_ref[...] = q * SCALE
    low = lanes_of((half_rows, LANES)) < HD
    for block in range(2):
        at, width = block * half_rows, (block + 1) * n_keys // 2
        chosen = both_heads(rope_ref[at : at + half_rows, :], low)
        scores = contract(key_ref[:width, :], chosen, (1, 1))
        causal = key_place_ref[:width, :] <= place_ref[block : block + 1, :]
        scores = jnp.where(causal, scores, -1e30)
        peak = jnp.max(scores, 0, keepdims=True)
        expo = jnp.exp(scores - peak)
        total = jnp.sum(expo, 0, keepdims=True)
        probs = (expo * (1.0 / total)).astype(bf16)
        out = contract(turned_ref[:, :width], probs, (1, 0)).T
        mixed_ref[at : at + half_rows, :] = jnp.where(
            low, out[:half_rows], out[half_rows:]
        ).astype(bf16)
        lse_ref[0, block : block + 1, :] = peak + jnp.log(total)


def attend(q, kv, cosine, sine, places, key_places):
    rows, cols = q.shape
    n_keys, kv_cols = kv.shape
    pairs, kv_heads = cols // LANES, kv_cols // LANES
    per_head = pairs // kv_heads
    whole = pl.BlockSpec((rows, LANES), lambda p: (0, 0))
    column = pl.BlockSpec((rows, LANES), lambda p: (0, p))
    return pl.pallas_call(
        functools.partial(attend_kernel, per_head),
        grid=(pairs,),
        in_specs=[
            column,
            pl.BlockSpec((n_keys, LANES), lambda p: (0, p // per_head)),
            whole,
            whole,
            pl.BlockSpec((2, rows), lambda p: (0, 0)),
            pl.BlockSpec((n_keys, 1), lambda p: (0, 0)),
        ],
        out_specs=[column, column, pl.BlockSpec((1, 2, rows), lambda p: (p, 0, 0))],
        out_shape=[
            jax.ShapeDtypeStruct((rows, cols), bf16),
            jax.ShapeDtypeStruct((rows, cols), bf16),
            jax.ShapeDtypeStruct((pairs, 2, rows), f32),
        ],
        scratch_shapes=[pltpu.VMEM((n_keys, LANES), bf16), pltpu.VMEM((LANES, n_keys), bf16)],
        compiler_params=pltpu.CompilerParams(
            dimension_semantics=("arbitrary",), vmem_limit_bytes=VMEM_LIMIT
        ),
        name="attend",
    )(q, kv, cosine, sine, places, key_places)


def attend_back_kernel(
    per_head, q_ref, kv_ref, lse_ref, grad_ref, cos_ref, sin_ref, place_ref, key_place_ref,
    dq_ref, dkv_ref, key_ref, value_ref, turned_ref, dk_acc, dv_acc,
):
    rows = q_ref.shape[0]
    half_rows, n_keys = rows // 2, kv_ref.shape[0]
    step = pl.program_id(0)
    load_keys(step, per_head, kv_ref, key_ref, value_ref, turned_ref, True)

    @pl.when(step % per_head == 0)
    def _():
        dk_acc[...] = jnp.zeros_like(dk_acc)
        dv_acc[...] = jnp.zeros_like(dv_acc)

    lane = lanes_of((half_rows, LANES))
    low = lane < HD
    for block in range(2):
        at, width = block * half_rows, (block + 1) * n_keys // 2
        chosen = both_heads(q_ref[at : at + half_rows, :], low)
        grad = both_heads(grad_ref[at : at + half_rows, :], low)
        keys, values = key_ref[:width, :], value_ref[:width, :]
        scores = contract(keys, chosen, (1, 1))
        causal = key_place_ref[:width, :] <= place_ref[block : block + 1, :]
        probs = jnp.where(causal, jnp.exp(scores - lse_ref[0, block : block + 1, :]), 0.0)
        prob_grad = contract(values, grad, (1, 1))
        inner = jnp.sum(probs * prob_grad, 0, keepdims=True)
        score_grad = (probs * (prob_grad - inner)).astype(bf16)
        dk_acc[:width, :] += contract(score_grad, chosen, (1, 0))
        dv_acc[:width, :] += contract(probs.astype(bf16), grad, (1, 0))
        out = SCALE * contract(turned_ref[:, :width], score_grad, (1, 0)).T
        total = jnp.where(low, out[:half_rows], out[half_rows:])
        dq_ref[at : at + half_rows, :] = (
            total * cos_ref[at : at + half_rows, :]
            - swap_halves(total, lane) * sin_ref[at : at + half_rows, :]
        ).astype(bf16)

    @pl.when(step % per_head == per_head - 1)
    def _():
        dk, dv = dk_acc[...], dv_acc[...]
        dk = dk + pltpu.roll(dk, HD, 1)
        dv = dv + pltpu.roll(dv, HD, 1)
        dkv_ref[...] = jnp.where(lanes_of(dk.shape) < HD, dk, dv).astype(bf16)


def attend_back(rope, kv, lse, grad, cosine, sine, places, key_places):
    rows, cols = rope.shape
    n_keys, kv_cols = kv.shape
    pairs, kv_heads = cols // LANES, kv_cols // LANES
    per_head = pairs // kv_heads
    whole = pl.BlockSpec((rows, LANES), lambda p: (0, 0))
    column = pl.BlockSpec((rows, LANES), lambda p: (0, p))
    keys = pl.BlockSpec((n_keys, LANES), lambda p: (0, p // per_head))
    return pl.pallas_call(
        functools.partial(attend_back_kernel, per_head),
        grid=(pairs,),
        in_specs=[
            column,
            keys,
            pl.BlockSpec((1, 2, rows), lambda p: (p, 0, 0)),
            column,
            whole,
            whole,
            pl.BlockSpec((2, rows), lambda p: (0, 0)),
            pl.BlockSpec((n_keys, 1), lambda p: (0, 0)),
        ],
        out_specs=[column, keys],
        out_shape=[
            jax.ShapeDtypeStruct((rows, cols), bf16),
            jax.ShapeDtypeStruct((n_keys, kv_cols), bf16),
        ],
        scratch_shapes=[
            pltpu.VMEM((n_keys, LANES), bf16),
            pltpu.VMEM((n_keys, LANES), bf16),
            pltpu.VMEM((LANES, n_keys), bf16),
            pltpu.VMEM((n_keys, LANES), f32),
            pltpu.VMEM((n_keys, LANES), f32),
        ],
        compiler_params=pltpu.CompilerParams(
            dimension_semantics=("arbitrary",), vmem_limit_bytes=VMEM_LIMIT
        ),
        name="attend_back",
    )(rope, kv, lse, grad, cosine, sine, places, key_places)


def ring(x, hop):
    size = lax.axis_size("mp")
    return lax.ppermute(x, "mp", [(k, (k + hop) % size) for k in range(size)])


def ring_gather(shard):
    return [shard] + [ring(shard, hop) for hop in range(1, lax.axis_size("mp"))]


def ring_scatter(pieces):
    total = pieces[0].astype(f32)
    for hop in range(1, len(pieces)):
        total = total + ring(pieces[hop], -hop).astype(f32)
    return total


def tie(values, filler):
    return lax.optimization_barrier((values, filler))


def piece_order():
    size = lax.axis_size("mp")
    order = []
    for step in range(1, size // 2 + 1):
        order += [step, size - step] if 2 * step < size else [step]
    return order + [0]


def line_gather(shard):
    size = lax.axis_size("mp")
    me = lax.axis_index("mp")
    ups, downs = [shard], [shard]
    for step in range(1, size):
        ups.append(lax.ppermute(ups[-1], "mp", [(k, k + 1) for k in range(step - 1, size - 1)]))
        downs.append(lax.ppermute(downs[-1], "mp", [(k + 1, k) for k in range(size - step)]))
    pieces = [shard] + [
        jnp.where(me >= hop, ups[hop], downs[size - hop]) for hop in range(1, size)
    ]
    return jnp.concatenate([pieces[i] for i in piece_order()])


def arrivals(shard):
    size = lax.axis_size("mp")
    me = lax.axis_index("mp")
    yield me, shard
    up, downs = shard, [shard]
    for step in range(1, size):
        up = lax.ppermute(up, "mp", [(k, k + 1) for k in range(step - 1, size - 1)])
        downs.append(lax.ppermute(downs[-1], "mp", [(k + 1, k) for k in range(size - step)]))
        piece = up
        for place in range(step):
            piece = jnp.where(me == place, downs[step - place], piece)
        yield jnp.where(me >= step, me - step, step), piece


def line_scatter(parts, fillers=()):
    size = lax.axis_size("mp")
    split = []
    for part in parts:
        split += list(part.reshape((size // len(parts), -1) + part.shape[1:]))
    piece = dict(zip(piece_order(), split))
    fillers = list(fillers)
    up, down = None, None
    for step in range(1, size):
        mine_up, mine_down = piece[step], piece[size - step]
        if step > 1:
            mine_up, mine_down = mine_up + up, mine_down + down
        up = lax.ppermute(mine_up, "mp", [(k, k + 1) for k in range(min(step, size - 1))])
        down = lax.ppermute(
            mine_down, "mp", [(k + 1, k) for k in range(max(size - 1 - step, 0), size - 1)]
        )
        if step <= len(fillers):
            (up, down), fillers[step - 1] = tie((up, down), fillers[step - 1])
    return piece[0].astype(f32) + up.astype(f32) + down.astype(f32), fillers


def halves(x):
    n = x.shape[0] // 2
    return [x[:n], x[n:]]


def adamw(weight, grad, mean_old, square_old, factor, rate, decay):
    clipped = grad.astype(f32) * factor
    mean_new = BETA_ONE * mean_old + (1 - BETA_ONE) * clipped
    square_new = BETA_TWO * square_old + (1 - BETA_TWO) * clipped * clipped
    ratio = (
        mean_new / (1 - BETA_ONE**STEP) / (jnp.sqrt(square_new / (1 - BETA_TWO**STEP)) + ADAM_EPS)
    )
    return (weight - rate * (ratio + decay * weight), mean_new, square_new)


def dot(a, b, dims=((1,), (0,)), out=f32):
    return lax.dot_general(a, b, (dims, ((), ())), preferred_element_type=f32).astype(out)


def body(
    tokens,
    targets,
    select,
    bucket,
    embed_table,
    query_weight,
    keyvalue_weight,
    output_weight,
    gateup_weight,
    down_weight,
    head_weight,
    norm_gains,
    embed_mean,
    query_mean,
    keyvalue_mean,
    output_mean,
    gateup_mean,
    down_mean,
    head_mean,
    gains_mean,
    embed_square,
    query_square,
    keyvalue_square,
    output_square,
    gateup_square,
    down_square,
    head_square,
    gains_square,
):
    n_dp, n_mp = lax.axis_size("dp"), lax.axis_size("mp")
    group = lax.axis_index("mp")
    rows = tokens.shape[0]
    home = rows // n_mp
    strip = home // 2
    table_rows, table_cols = embed_table.shape
    vocab_start = group * table_rows
    kv_cols = keyvalue_weight.shape[1]
    q_cols = query_weight.shape[1]
    ring_order = (group - jnp.arange(n_mp)) % n_mp
    line_order = (group - jnp.array(piece_order())) % n_mp

    def by_piece(x, order):
        strips = x.reshape(x.shape[:-1] + (2 * n_mp, strip))
        first = strips[..., order, :]
        second = strips[..., 2 * n_mp - 1 - order, :]
        return jnp.concatenate([first, second], -1)

    def pair_heads(x):
        return x.reshape(-1, 2, KVH, HD).transpose(0, 2, 1, 3).reshape(-1, kv_cols)

    scales_int = select * bucket
    meta = jnp.concatenate(
        [tokens.astype(f32), scales_int.astype(f32), norm_gains.astype(bf16).astype(f32).reshape(-1)]
    )
    meta = lax.all_gather(meta, "dp")
    ids = meta[:, :rows].astype(jnp.int32)
    gains_rows = meta[:, 2 * rows :].reshape(n_dp, 3, -1).transpose(1, 0, 2).reshape(3, -1)

    def ordered(pieces, axis):
        stacked = jnp.stack(pieces)
        return jnp.concatenate([stacked[(group - k) % n_mp] for k in range(n_mp)], axis)

    weight_total = jnp.sum(meta[:, rows : 2 * rows])
    ids_local = by_piece(ids, line_order).transpose(1, 0, 2) - vocab_start

    def look_up(piece_ids):
        inside = (piece_ids >= 0) & (piece_ids < table_rows)
        found = embed_table[jnp.clip(piece_ids, 0, table_rows - 1)]
        return jnp.where(inside[:, None], found, 0.0).astype(bf16)

    looked = look_up(ids_local.reshape(-1))

    (query_own, output_own), meta = tie(
        (query_weight.astype(bf16), output_weight.astype(bf16)), meta
    )
    query_pieces, output_pieces = ring_gather(query_own), ring_gather(output_own)
    looked, (query_pieces, output_pieces) = tie(looked, (query_pieces, output_pieces))
    kvq_own = jnp.concatenate(
        [pair_heads(keyvalue_weight.astype(bf16)), ordered(query_pieces, 1)], 1
    )
    kvq_full = lax.all_gather(kvq_own, "dp", axis=0, tiled=True)
    looked, (gateup_own, down_own, head_own) = line_scatter(
        [looked],
        [
            gateup_weight.astype(bf16).transpose(1, 0, 2).reshape(table_cols, -1),
            down_weight.astype(bf16),
            head_weight.astype(bf16),
        ],
    )
    output_own = ordered(output_pieces, 0)
    gateup_full = lax.all_gather(gateup_own, "dp", axis=0, tiled=True)
    output_full = lax.all_gather(output_own, "dp", axis=1, tiled=True)
    down_full = lax.all_gather(down_own, "dp", axis=1, tiled=True)
    head_full = lax.all_gather(head_own, "dp", axis=0, tiled=True)

    positions = by_piece(jnp.arange(rows), ring_order)
    cosine, sine = rotary_tables(positions[0])
    key_places = jnp.concatenate([positions[:, :strip].reshape(-1), positions[:, strip:].reshape(-1)])
    places, key_places = jnp.tile(positions[0].reshape(2, strip), (1, 2)), key_places[:, None]

    looked = looked.astype(bf16)
    looked = lax.all_to_all(looked.reshape(n_dp, home, table_cols), "dp", 0, 0)
    start_rows = looked.transpose(1, 0, 2).reshape(home, -1).astype(f32)

    first_in = normed(start_rows, gains_rows[0]).astype(bf16)
    kv_own = turn_keys(dot(first_in, kvq_full[:, :kv_cols]), cosine, sine, 1.0, KVH)
    queries = dot(first_in, kvq_full[:, kv_cols:])
    kv_pieces = ring_gather(kv_own)
    kv = jnp.concatenate([p[:strip] for p in kv_pieces] + [p[strip:] for p in kv_pieces])
    mixed, rope, lse = attend(queries, kv, cosine, sine, places, key_places)
    middle_rows = start_rows + dot(mixed, output_full)

    second_in = line_gather(normed(middle_rows, gains_rows[1]).astype(bf16))
    gate_upper = dot(second_in, gateup_full)
    half = gate_upper.shape[1] // 2
    gate, upper = gate_upper[:, :half], gate_upper[:, half:]
    active = (jax.nn.silu(gate) * upper).astype(bf16)
    final_rows = middle_rows + line_scatter([dot(a, down_full, out=bf16) for a in halves(active)])[0]

    final_in = line_gather(normed(final_rows, gains_rows[2]).astype(bf16))
    head_cols = head_full.shape[1]
    goals = by_piece(targets, line_order).reshape(-1) - group * head_cols
    scales = by_piece(scales_int, line_order).reshape(-1).astype(f32)
    logits = dot(final_in, head_full)
    hits = jnp.arange(head_cols)[None, :] == goals[:, None]
    local_top = jnp.max(logits, -1)
    stats = jnp.stack(
        [
            local_top,
            jnp.sum(jnp.exp(logits - local_top[:, None]), -1),
            jnp.sum(jnp.where(hits, logits, 0.0), -1),
        ]
    ).reshape(3, n_mp, home)
    back = [piece_order().index(i) for i in range(n_mp)]
    stats = stats[:, jnp.array(back)[ring_order]]
    stats = jnp.stack(ring_gather(stats))[:, :, line_order].reshape(n_mp, 3, rows)
    top = jnp.max(stats[:, 0], 0)
    expsum = jnp.sum(stats[:, 1] * jnp.exp(stats[:, 0] - top[None]), 0)
    logsum_all = top + jnp.log(expsum)
    picked = jnp.sum(stats[:, 2], 0)
    loss_part = jnp.sum(scales * (logsum_all - picked)) / n_mp
    coef = scales * (1.0 / weight_total)
    logit_grad = (
        (jnp.exp(logits - logsum_all[:, None]) - hits.astype(f32)) * coef[:, None]
    ).astype(bf16)

    def reduce_to(grad, axis):
        return lax.psum_scatter(grad, "dp", scatter_dimension=axis, tiled=True)

    head_full, head_grad = tie(head_full, dot(final_in, logit_grad, ((0,), (0,)), bf16))
    final_grad, _ = line_scatter([dot(logit_grad, head_full, ((1,), (1,)), bf16)])
    head_part = reduce_to(head_grad, 0)
    residual, final_gain = norm_back(final_rows, gains_rows[2], final_grad)

    branch = line_gather(residual.astype(bf16))
    sigmoid = jax.nn.sigmoid(gate)
    silu_gate = gate * sigmoid
    active_grad = dot(branch, down_full, ((1,), (1,)))
    gate_grad = (active_grad * upper * sigmoid * (1.0 + gate * (1.0 - sigmoid))).astype(bf16)
    upper_grad = (active_grad * silu_gate).astype(bf16)
    gateup_grad = jnp.concatenate([gate_grad, upper_grad], 1)
    second_partial = [dot(g, gateup_full, ((1,), (1,)), bf16) for g in halves(gateup_grad)]
    second_grad, (down_grad, gateup_w) = line_scatter(
        second_partial,
        [
            dot(active, branch, ((0,), (0,)), bf16),
            dot(second_in, gateup_grad, ((0,), (0,)), bf16),
        ],
    )
    down_grad, head_part = tie(down_grad, head_part)
    down_part = reduce_to(down_grad, 1)
    second_grad, down_part = tie(second_grad, down_part)
    gateup_part = reduce_to(gateup_w, 0)
    middle_extra, middle_gain = norm_back(middle_rows, gains_rows[1], second_grad)
    residual = residual + middle_extra

    branch = residual.astype(bf16)
    place = lax.axis_index("dp")
    by_owner = branch.reshape(home, n_dp // 2, 2, table_cols)

    def columns_for(parity):
        return lax.dynamic_index_in_dim(by_owner, parity, 2, False).reshape(home, -1)

    given = dot(mixed, columns_for(1 - place % 2), ((0,), (0,)), bf16)
    kept = dot(mixed, columns_for(place % 2), ((0,), (0,)), bf16)
    branch, (given, kept) = tie(branch, (given, kept))
    taken = lax.ppermute(given, "dp", [(k, k ^ 1) for k in range(n_dp)])

    def owner_columns(hop):
        at = ((place // 2) ^ hop) * table_cols
        return (
            lax.dynamic_slice_in_dim(kept, at, table_cols, 1).astype(f32)
            + lax.dynamic_slice_in_dim(taken, at, table_cols, 1).astype(f32)
        )

    output_w = [owner_columns(0)]
    for hop in range(1, n_dp // 2):
        output_w.append(
            lax.ppermute(
                owner_columns(hop).astype(bf16), "dp", [(k, k ^ (2 * hop)) for k in range(n_dp)]
            )
        )
    mixed_grad = dot(branch, output_full, ((1,), (1,)), bf16)
    query_pre, kv_grad = attend_back(rope, kv, lse, mixed_grad, cosine, sine, places, key_places)
    kv_halves = kv_grad.reshape(2, n_mp, strip, kv_cols)
    kv_grad = ring_scatter([jnp.concatenate([kv_halves[0, i], kv_halves[1, i]]) for i in range(n_mp)])
    pair_grad = turn_keys(kv_grad, cosine, sine, -1.0, KVH)
    kvq_grad = jnp.concatenate([pair_grad, query_pre], 1)
    kvq_grad, kvq_w = tie(kvq_grad, dot(first_in, kvq_grad, ((0,), (0,)), bf16))
    first_grad = dot(kvq_grad, kvq_full, ((1,), (1,)))
    start_extra, start_gain = norm_back(start_rows, gains_rows[0], first_grad)
    start_grad = (residual + start_extra).astype(bf16)
    gains_grad = jnp.stack([start_gain, middle_gain, final_gain]).astype(bf16)

    def piece_of(x, hop, axis, length):
        return lax.dynamic_slice_in_dim(x, (group - hop) % n_mp * length, length, axis)

    moved = jnp.concatenate([start_grad, gains_grad, jnp.zeros((13, start_grad.shape[1]), bf16)])
    moved = moved.reshape(-1, n_dp, table_cols).transpose(1, 0, 2)
    moved = lax.all_to_all(moved, "dp", 0, 0)
    kvq_w, gateup_part = tie(kvq_w, gateup_part)
    kvq_w = reduce_to(kvq_w, 0)
    gateup_part = gateup_part.reshape(table_cols, 2, half).transpose(1, 0, 2)
    gains_part = ring_scatter([jnp.sum(moved[:, home : home + 3].astype(f32), 0)] * n_mp)
    embed_part = None
    ids_home = by_piece(ids, jnp.arange(n_mp)).transpose(1, 0, 2).reshape(n_mp, -1) - vocab_start
    for number, (device, shard) in enumerate(
        arrivals(moved[:, :home].reshape(n_dp * home, table_cols))
    ):
        onehot = (ids_home[device][None, :] == jnp.arange(table_rows)[:, None]).astype(bf16)
        part = dot(onehot, shard)
        embed_part = part if embed_part is None else embed_part + part
        if number == n_mp // 2:
            output_w, embed_part = tie(output_w, embed_part)
            output_w = sum(piece.astype(f32) for piece in output_w).astype(bf16)

    query_part = ring_scatter(
        [piece_of(kvq_w[:, kv_cols:], i, 1, q_cols) for i in range(n_mp)]
    )
    kv_rows = table_cols // n_mp
    keyvalue_part = ring_scatter([piece_of(kvq_w[:, :kv_cols], i, 0, kv_rows) for i in range(n_mp)])
    keyvalue_part = ordered(ring_gather(keyvalue_part), 0)
    keyvalue_part = keyvalue_part.reshape(-1, KVH, 2, HD).transpose(0, 2, 1, 3).reshape(-1, kv_cols)
    output_part = ring_scatter(
        [piece_of(output_w, i, 0, output_weight.shape[0]) for i in range(n_mp)]
    )

    leading = (group == 0).astype(f32)

    def square(piece):
        piece = piece.astype(f32)
        return jnp.sum(piece * piece)

    squared = sum(
        square(piece)
        for piece in (embed_part, query_part, output_part, gateup_part, down_part, head_part)
    )
    squared = squared + leading * (square(keyvalue_part) + square(gains_part))
    totals = jnp.stack([squared, loss_part])[:, None]
    totals = sum(ring_gather(totals))
    hop = 1
    while hop < n_dp:
        totals = totals + lax.ppermute(totals, "dp", [(k, k ^ hop) for k in range(n_dp)])
        hop *= 2
    grad_norm, loss_sum = jnp.sqrt(totals[0, 0]), totals[1, 0]
    factor = jnp.minimum(1.0, CLIP / (grad_norm + 1e-06))
    outs = [loss_sum, weight_total, grad_norm]
    for number, (weight, grad, mean_old, square_old) in enumerate(
        (
            (embed_table, embed_part, embed_mean, embed_square),
            (query_weight, query_part, query_mean, query_square),
            (keyvalue_weight, keyvalue_part, keyvalue_mean, keyvalue_square),
            (output_weight, output_part, output_mean, output_square),
            (gateup_weight, gateup_part, gateup_mean, gateup_square),
            (down_weight, down_part, down_mean, down_square),
            (head_weight, head_part, head_mean, head_square),
            (norm_gains, gains_part, gains_mean, gains_square),
        )
    ):
        new, mean_new, square_new = adamw(
            weight, grad, mean_old, square_old, factor, RATES[number], DECAYS[number]
        )
        outs += [new, embed_part * factor if number == 0 else mean_new, square_new]
    return tuple(outs)


def solution(mesh):
    weights = (
        P("mp", "dp"),
        P("dp", "mp"),
        P("dp", None),
        P("mp", "dp"),
        P(None, "dp", "mp"),
        P("mp", "dp"),
        P("dp", "mp"),
        P(None, "dp"),
    )
    in_specs = (P("dp"),) * 4 + weights * 3
    out_specs = (P(),) * 3 + tuple(spec for spec in weights for _ in range(3))
    return jax.shard_map(body, mesh=mesh, in_specs=in_specs, out_specs=out_specs, check_vma=False)
```

```python
import functools

import jax
import jax.numpy as jnp
from jax import lax
from jax.experimental import pallas as pl
from jax.experimental.pallas import tpu as pltpu
from jax.sharding import PartitionSpec as P

HD = 64
KVH = 4
LEN = 1024
STEP = 5

EPS = 1e-05
SCALE = 0.125
CLIP = 0.01
BETA_ONE = 0.9
BETA_TWO = 0.95
ADAM_EPS = 1e-08
RATES = (0.9, 0.01, 0.01, 0.06, 0.01, 0.01, 0.08, 0.9)
DECAYS = (0.1, 0.1, 0.1, 0.1, 0.1, 0.1, 0.1, 0.0)

LANES = 128
VMEM_LIMIT = 56 * 1024 * 1024

f32 = jnp.float32
bf16 = jnp.bfloat16


def normed(hidden, gain):
    return hidden * lax.rsqrt(jnp.mean(hidden * hidden, axis=-1, keepdims=True) + EPS) * gain


def norm_back(hidden, gain, upstream):
    _, pullback = jax.vjp(normed, hidden, gain)
    return pullback(upstream)


def rotary_tables(places):
    freqs = 10000.0 ** (-(2 * jnp.arange(HD // 2)).astype(f32) / HD)
    angles = (places % LEN).astype(f32)[:, None] * freqs[None, :]
    cosine = jnp.cos(angles)
    sine = jnp.sin(angles)
    return (
        jnp.concatenate([cosine] * 4, -1),
        jnp.concatenate([-sine, sine, -sine, sine], -1),
    )


def swap_halves(x, lane):
    half = HD // 2
    return jnp.where(
        lane % HD < half, pltpu.roll(x, LANES - half, 1), pltpu.roll(x, half, 1)
    )


def lanes_of(shape):
    return lax.broadcasted_iota(jnp.int32, shape, 1)


def turn_kernel(sign, kv_ref, cos_ref, sin_ref, out_ref):
    rows = kv_ref.shape[0]
    lane = lanes_of((rows, LANES))
    x = kv_ref[...]
    turned = x * cos_ref[...] + sign * swap_halves(x, lane) * sin_ref[...]
    out_ref[...] = jnp.where(lane < HD, turned, x).astype(bf16)


def turn_keys(kv, cosine, sine, sign, n_heads):
    rows = kv.shape[0]
    column = pl.BlockSpec((rows, LANES), lambda p: (0, p))
    whole = pl.BlockSpec((rows, LANES), lambda p: (0, 0))
    return pl.pallas_call(
        functools.partial(turn_kernel, sign),
        grid=(n_heads,),
        in_specs=[column, whole, whole],
        out_specs=column,
        out_shape=jax.ShapeDtypeStruct((rows, n_heads * LANES), bf16),
        name="turn_keys",
    )(kv, cosine, sine)


def load_keys(step, per_head, kv_ref, key_ref, value_ref, turned_ref, turn_key):
    @pl.when(step % per_head == 0)
    def _():
        pair = kv_ref[...].astype(f32)
        other = pltpu.roll(pair, HD, 1)
        lane = lanes_of(pair.shape)
        key = jnp.where(lane < HD, pair, other)
        value = jnp.where(lane < HD, other, pair)
        key_ref[...] = key.astype(bf16)
        if value_ref is not None:
            value_ref[...] = value.astype(bf16)
        turned_ref[...] = (key if turn_key else value).T.astype(bf16)


def both_heads(pair, low):
    zero = jnp.zeros_like(pair)
    return jnp.concatenate([jnp.where(low, pair, zero), jnp.where(low, zero, pair)])


def contract(a, b, dims):
    return lax.dot_general(a, b, (((dims[0],), (dims[1],)), ((), ())), preferred_element_type=f32)


def attend_kernel(
    per_head, q_ref, kv_ref, cos_ref, sin_ref, place_ref, key_place_ref,
    mixed_ref, rope_ref, lse_ref, key_ref, turned_ref,
):
    rows = q_ref.shape[0]
    half_rows, n_keys = rows // 2, kv_ref.shape[0]
    load_keys(pl.program_id(0), per_head, kv_ref, key_ref, None, turned_ref, False)
    q = q_ref[...]
    q = (q * cos_ref[...] + swap_halves(q, lanes_of(q.shape)) * sin_ref[...]).astype(bf16)
    rope_ref[...] = q * SCALE
    low = lanes_of((half_rows, LANES)) < HD
    for block in range(2):
        at, width = block * half_rows, (block + 1) * n_keys // 2
        chosen = both_heads(rope_ref[at : at + half_rows, :], low)
        scores = contract(key_ref[:width, :], chosen, (1, 1))
        causal = key_place_ref[:width, :] <= place_ref[block : block + 1, :]
        scores = jnp.where(causal, scores, -1e30)
        peak = jnp.max(scores, 0, keepdims=True)
        expo = jnp.exp(scores - peak)
        total = jnp.sum(expo, 0, keepdims=True)
        probs = (expo * (1.0 / total)).astype(bf16)
        out = contract(turned_ref[:, :width], probs, (1, 0)).T
        mixed_ref[at : at + half_rows, :] = jnp.where(
            low, out[:half_rows], out[half_rows:]
        ).astype(bf16)
        lse_ref[0, block : block + 1, :] = peak + jnp.log(total)


def attend(q, kv, cosine, sine, places, key_places):
    rows, cols = q.shape
    n_keys, kv_cols = kv.shape
    pairs, kv_heads = cols // LANES, kv_cols // LANES
    per_head = pairs // kv_heads
    whole = pl.BlockSpec((rows, LANES), lambda p: (0, 0))
    column = pl.BlockSpec((rows, LANES), lambda p: (0, p))
    return pl.pallas_call(
        functools.partial(attend_kernel, per_head),
        grid=(pairs,),
        in_specs=[
            column,
            pl.BlockSpec((n_keys, LANES), lambda p: (0, p // per_head)),
            whole,
            whole,
            pl.BlockSpec((2, rows), lambda p: (0, 0)),
            pl.BlockSpec((n_keys, 1), lambda p: (0, 0)),
        ],
        out_specs=[column, column, pl.BlockSpec((1, 2, rows), lambda p: (p, 0, 0))],
        out_shape=[
            jax.ShapeDtypeStruct((rows, cols), bf16),
            jax.ShapeDtypeStruct((rows, cols), bf16),
            jax.ShapeDtypeStruct((pairs, 2, rows), f32),
        ],
        scratch_shapes=[pltpu.VMEM((n_keys, LANES), bf16), pltpu.VMEM((LANES, n_keys), bf16)],
        compiler_params=pltpu.CompilerParams(
            dimension_semantics=("arbitrary",), vmem_limit_bytes=VMEM_LIMIT
        ),
        name="attend",
    )(q, kv, cosine, sine, places, key_places)


def attend_back_kernel(
    per_head, q_ref, kv_ref, lse_ref, grad_ref, cos_ref, sin_ref, place_ref, key_place_ref,
    dq_ref, dkv_ref, key_ref, value_ref, turned_ref, dk_acc, dv_acc,
):
    rows = q_ref.shape[0]
    half_rows, n_keys = rows // 2, kv_ref.shape[0]
    step = pl.program_id(0)
    load_keys(step, per_head, kv_ref, key_ref, value_ref, turned_ref, True)

    @pl.when(step % per_head == 0)
    def _():
        dk_acc[...] = jnp.zeros_like(dk_acc)
        dv_acc[...] = jnp.zeros_like(dv_acc)

    lane = lanes_of((half_rows, LANES))
    low = lane < HD
    for block in range(2):
        at, width = block * half_rows, (block + 1) * n_keys // 2
        chosen = both_heads(q_ref[at : at + half_rows, :], low)
        grad = both_heads(grad_ref[at : at + half_rows, :], low)
        keys, values = key_ref[:width, :], value_ref[:width, :]
        scores = contract(keys, chosen, (1, 1))
        causal = key_place_ref[:width, :] <= place_ref[block : block + 1, :]
        probs = jnp.where(causal, jnp.exp(scores - lse_ref[0, block : block + 1, :]), 0.0)
        prob_grad = contract(values, grad, (1, 1))
        inner = jnp.sum(probs * prob_grad, 0, keepdims=True)
        score_grad = (probs * (prob_grad - inner)).astype(bf16)
        dk_acc[:width, :] += contract(score_grad, chosen, (1, 0))
        dv_acc[:width, :] += contract(probs.astype(bf16), grad, (1, 0))
        out = SCALE * contract(turned_ref[:, :width], score_grad, (1, 0)).T
        total = jnp.where(low, out[:half_rows], out[half_rows:])
        dq_ref[at : at + half_rows, :] = (
            total * cos_ref[at : at + half_rows, :]
            - swap_halves(total, lane) * sin_ref[at : at + half_rows, :]
        ).astype(bf16)

    @pl.when(step % per_head == per_head - 1)
    def _():
        dk, dv = dk_acc[...], dv_acc[...]
        dk = dk + pltpu.roll(dk, HD, 1)
        dv = dv + pltpu.roll(dv, HD, 1)
        dkv_ref[...] = jnp.where(lanes_of(dk.shape) < HD, dk, dv).astype(bf16)


def attend_back(rope, kv, lse, grad, cosine, sine, places, key_places):
    rows, cols = rope.shape
    n_keys, kv_cols = kv.shape
    pairs, kv_heads = cols // LANES, kv_cols // LANES
    per_head = pairs // kv_heads
    whole = pl.BlockSpec((rows, LANES), lambda p: (0, 0))
    column = pl.BlockSpec((rows, LANES), lambda p: (0, p))
    keys = pl.BlockSpec((n_keys, LANES), lambda p: (0, p // per_head))
    return pl.pallas_call(
        functools.partial(attend_back_kernel, per_head),
        grid=(pairs,),
        in_specs=[
            column,
            keys,
            pl.BlockSpec((1, 2, rows), lambda p: (p, 0, 0)),
            column,
            whole,
            whole,
            pl.BlockSpec((2, rows), lambda p: (0, 0)),
            pl.BlockSpec((n_keys, 1), lambda p: (0, 0)),
        ],
        out_specs=[column, keys],
        out_shape=[
            jax.ShapeDtypeStruct((rows, cols), bf16),
            jax.ShapeDtypeStruct((n_keys, kv_cols), bf16),
        ],
        scratch_shapes=[
            pltpu.VMEM((n_keys, LANES), bf16),
            pltpu.VMEM((n_keys, LANES), bf16),
            pltpu.VMEM((LANES, n_keys), bf16),
            pltpu.VMEM((n_keys, LANES), f32),
            pltpu.VMEM((n_keys, LANES), f32),
        ],
        compiler_params=pltpu.CompilerParams(
            dimension_semantics=("arbitrary",), vmem_limit_bytes=VMEM_LIMIT
        ),
        name="attend_back",
    )(rope, kv, lse, grad, cosine, sine, places, key_places)


def ring(x, hop):
    size = lax.axis_size("mp")
    return lax.ppermute(x, "mp", [(k, (k + hop) % size) for k in range(size)])


def ring_gather(shard):
    return [shard] + [ring(shard, hop) for hop in range(1, lax.axis_size("mp"))]


def ring_scatter(pieces):
    total = pieces[0].astype(f32)
    for hop in range(1, len(pieces)):
        total = total + ring(pieces[hop], -hop).astype(f32)
    return total


def tie(values, filler):
    return lax.optimization_barrier((values, filler))


def piece_order():
    size = lax.axis_size("mp")
    order = []
    for step in range(1, size // 2 + 1):
        order += [step, size - step] if 2 * step < size else [step]
    return order + [0]


def relay(ups, downs):
    size, step = lax.axis_size("mp"), len(ups)
    ups.append(lax.ppermute(ups[-1], "mp", [(k, k + 1) for k in range(step - 1, size - 1)]))
    downs.append(lax.ppermute(downs[-1], "mp", [(k + 1, k) for k in range(size - step)]))


def relay_tied(value, ups, downs, last=False):
    relay(ups, downs)
    while last and len(ups) < lax.axis_size("mp"):
        relay(ups, downs)
    value, (ups[-1], downs[-1]) = tie(value, (ups[-1], downs[-1]))
    return value


def line_pieces(ups, downs):
    size, me = len(ups), lax.axis_index("mp")
    pieces = [ups[0]] + [
        jnp.where(me >= hop, ups[hop], downs[size - hop]) for hop in range(1, size)
    ]
    return jnp.concatenate([pieces[i] for i in piece_order()])


def line_gather(shard):
    ups, downs = [shard], [shard]
    while len(ups) < lax.axis_size("mp"):
        relay(ups, downs)
    return line_pieces(ups, downs)


def arrivals(shard):
    size = lax.axis_size("mp")
    me = lax.axis_index("mp")
    yield me, shard
    up, downs = shard, [shard]
    for step in range(1, size):
        up = lax.ppermute(up, "mp", [(k, k + 1) for k in range(step - 1, size - 1)])
        downs.append(lax.ppermute(downs[-1], "mp", [(k + 1, k) for k in range(size - step)]))
        piece = up
        for place in range(step):
            piece = jnp.where(me == place, downs[step - place], piece)
        yield jnp.where(me >= step, me - step, step), piece


def line_scatter(parts, fillers=()):
    size = lax.axis_size("mp")
    split = []
    for part in parts:
        split += list(part.reshape((size // len(parts), -1) + part.shape[1:]))
    piece = dict(zip(piece_order(), split))
    fillers = list(fillers)
    up, down = None, None
    for step in range(1, size):
        mine_up, mine_down = piece[step], piece[size - step]
        if step > 1:
            mine_up, mine_down = mine_up + up, mine_down + down
        up = lax.ppermute(mine_up, "mp", [(k, k + 1) for k in range(min(step, size - 1))])
        down = lax.ppermute(
            mine_down, "mp", [(k + 1, k) for k in range(max(size - 1 - step, 0), size - 1)]
        )
        if step <= len(fillers):
            (up, down), fillers[step - 1] = tie((up, down), fillers[step - 1])
    return piece[0].astype(f32) + up.astype(f32) + down.astype(f32), fillers


def halves(x):
    n = x.shape[0] // 2
    return [x[:n], x[n:]]


def adamw(weight, grad, mean_old, square_old, factor, rate, decay):
    clipped = grad.astype(f32) * factor
    mean_new = BETA_ONE * mean_old + (1 - BETA_ONE) * clipped
    square_new = BETA_TWO * square_old + (1 - BETA_TWO) * clipped * clipped
    ratio = (
        mean_new / (1 - BETA_ONE**STEP) / (jnp.sqrt(square_new / (1 - BETA_TWO**STEP)) + ADAM_EPS)
    )
    return (weight - rate * (ratio + decay * weight), mean_new, square_new)


def dot(a, b, dims=((1,), (0,)), out=f32):
    return lax.dot_general(a, b, (dims, ((), ())), preferred_element_type=f32).astype(out)


def body(
    tokens,
    targets,
    select,
    bucket,
    embed_table,
    query_weight,
    keyvalue_weight,
    output_weight,
    gateup_weight,
    down_weight,
    head_weight,
    norm_gains,
    embed_mean,
    query_mean,
    keyvalue_mean,
    output_mean,
    gateup_mean,
    down_mean,
    head_mean,
    gains_mean,
    embed_square,
    query_square,
    keyvalue_square,
    output_square,
    gateup_square,
    down_square,
    head_square,
    gains_square,
):
    n_dp, n_mp = lax.axis_size("dp"), lax.axis_size("mp")
    group = lax.axis_index("mp")
    rows = tokens.shape[0]
    home = rows // n_mp
    strip = home // 2
    table_rows, table_cols = embed_table.shape
    vocab_start = group * table_rows
    kv_cols = keyvalue_weight.shape[1]
    q_cols = query_weight.shape[1]
    ring_order = (group - jnp.arange(n_mp)) % n_mp
    line_order = (group - jnp.array(piece_order())) % n_mp

    def by_piece(x, order):
        strips = x.reshape(x.shape[:-1] + (2 * n_mp, strip))
        first = strips[..., order, :]
        second = strips[..., 2 * n_mp - 1 - order, :]
        return jnp.concatenate([first, second], -1)

    def pair_heads(x):
        return x.reshape(-1, 2, KVH, HD).transpose(0, 2, 1, 3).reshape(-1, kv_cols)

    scales_int = select * bucket
    meta = jnp.concatenate(
        [tokens.astype(f32), scales_int.astype(f32), norm_gains.astype(bf16).astype(f32).reshape(-1)]
    )
    meta = lax.all_gather(meta, "dp")
    ids = meta[:, :rows].astype(jnp.int32)
    gains_rows = meta[:, 2 * rows :].reshape(n_dp, 3, -1).transpose(1, 0, 2).reshape(3, -1)

    def ordered(pieces, axis):
        stacked = jnp.stack(pieces)
        return jnp.concatenate([stacked[(group - k) % n_mp] for k in range(n_mp)], axis)

    weight_total = jnp.sum(meta[:, rows : 2 * rows])
    ids_local = by_piece(ids, line_order).transpose(1, 0, 2) - vocab_start

    def look_up(piece_ids):
        inside = (piece_ids >= 0) & (piece_ids < table_rows)
        found = embed_table[jnp.clip(piece_ids, 0, table_rows - 1)]
        return jnp.where(inside[:, None], found, 0.0).astype(bf16)

    looked = look_up(ids_local.reshape(-1))

    (query_own, output_own), meta = tie(
        (query_weight.astype(bf16), output_weight.astype(bf16)), meta
    )
    query_pieces, output_pieces = ring_gather(query_own), ring_gather(output_own)
    looked, (query_pieces, output_pieces) = tie(looked, (query_pieces, output_pieces))
    kvq_own = jnp.concatenate(
        [pair_heads(keyvalue_weight.astype(bf16)), ordered(query_pieces, 1)], 1
    )
    kvq_full = lax.all_gather(kvq_own, "dp", axis=0, tiled=True)
    looked, (gateup_own, down_own, head_own) = line_scatter(
        [looked],
        [
            gateup_weight.astype(bf16).transpose(1, 0, 2).reshape(table_cols, -1),
            down_weight.astype(bf16),
            head_weight.astype(bf16),
        ],
    )
    output_own = ordered(output_pieces, 0)
    gateup_full = lax.all_gather(gateup_own, "dp", axis=0, tiled=True)
    output_full = lax.all_gather(output_own, "dp", axis=1, tiled=True)
    down_full = lax.all_gather(down_own, "dp", axis=1, tiled=True)
    head_full = lax.all_gather(head_own, "dp", axis=0, tiled=True)

    positions = by_piece(jnp.arange(rows), ring_order)
    cosine, sine = rotary_tables(positions[0])
    key_places = jnp.concatenate([positions[:, :strip].reshape(-1), positions[:, strip:].reshape(-1)])
    places, key_places = jnp.tile(positions[0].reshape(2, strip), (1, 2)), key_places[:, None]

    looked = looked.astype(bf16)
    looked = lax.all_to_all(looked.reshape(n_dp, home, table_cols), "dp", 0, 0)
    start_rows = looked.transpose(1, 0, 2).reshape(home, -1).astype(f32)

    first_in = normed(start_rows, gains_rows[0]).astype(bf16)
    kv_own = turn_keys(dot(first_in, kvq_full[:, :kv_cols]), cosine, sine, 1.0, KVH)
    queries = dot(first_in, kvq_full[:, kv_cols:])
    kv_pieces = ring_gather(kv_own)
    kv = jnp.concatenate([p[:strip] for p in kv_pieces] + [p[strip:] for p in kv_pieces])
    mixed, rope, lse = attend(queries, kv, cosine, sine, places, key_places)
    ups, downs = [first_in], [first_in]
    mixed = relay_tied(mixed, ups, downs)
    middle_rows = start_rows + dot(mixed, output_full)

    second_in = line_gather(normed(middle_rows, gains_rows[1]).astype(bf16))
    gate_upper = dot(second_in, gateup_full)
    half = gate_upper.shape[1] // 2
    gate, upper = gate_upper[:, :half], gate_upper[:, half:]
    active = (jax.nn.silu(gate) * upper).astype(bf16)
    final_rows = middle_rows + line_scatter([dot(a, down_full, out=bf16) for a in halves(active)])[0]

    final_in = line_gather(normed(final_rows, gains_rows[2]).astype(bf16))
    head_cols = head_full.shape[1]
    goals = by_piece(targets, line_order).reshape(-1) - group * head_cols
    scales = by_piece(scales_int, line_order).reshape(-1).astype(f32)
    logits = dot(final_in, head_full)
    hits = jnp.arange(head_cols)[None, :] == goals[:, None]
    local_top = jnp.max(logits, -1)
    stats = jnp.stack(
        [
            local_top,
            jnp.sum(jnp.exp(logits - local_top[:, None]), -1),
            jnp.sum(jnp.where(hits, logits, 0.0), -1),
        ]
    ).reshape(3, n_mp, home)
    back = [piece_order().index(i) for i in range(n_mp)]
    stats = stats[:, jnp.array(back)[ring_order]]
    stats = jnp.stack(ring_gather(stats))[:, :, line_order].reshape(n_mp, 3, rows)
    top = jnp.max(stats[:, 0], 0)
    expsum = jnp.sum(stats[:, 1] * jnp.exp(stats[:, 0] - top[None]), 0)
    logsum_all = top + jnp.log(expsum)
    picked = jnp.sum(stats[:, 2], 0)
    loss_part = jnp.sum(scales * (logsum_all - picked)) / n_mp
    coef = scales * (1.0 / weight_total)
    logit_grad = (
        (jnp.exp(logits - logsum_all[:, None]) - hits.astype(f32)) * coef[:, None]
    ).astype(bf16)

    def reduce_to(grad, axis):
        return lax.psum_scatter(grad, "dp", scatter_dimension=axis, tiled=True)

    head_grad = relay_tied(dot(final_in, logit_grad, ((0,), (0,)), bf16), ups, downs)
    head_full, head_grad = tie(head_full, head_grad)
    final_partial = relay_tied(
        dot(logit_grad, head_full, ((1,), (1,)), bf16), ups, downs, last=True
    )
    first_all = line_pieces(ups, downs)
    final_grad, _ = line_scatter([final_partial])
    head_part = reduce_to(head_grad, 0)
    residual, final_gain = norm_back(final_rows, gains_rows[2], final_grad)

    branch = line_gather(residual.astype(bf16))
    sigmoid = jax.nn.sigmoid(gate)
    silu_gate = gate * sigmoid
    active_grad = dot(branch, down_full, ((1,), (1,)))
    gate_grad = (active_grad * upper * sigmoid * (1.0 + gate * (1.0 - sigmoid))).astype(bf16)
    upper_grad = (active_grad * silu_gate).astype(bf16)
    gateup_grad = jnp.concatenate([gate_grad, upper_grad], 1)
    second_partial = [dot(g, gateup_full, ((1,), (1,)), bf16) for g in halves(gateup_grad)]
    second_grad, (down_grad, gateup_w) = line_scatter(
        second_partial,
        [
            dot(active, branch, ((0,), (0,)), bf16),
            dot(second_in, gateup_grad, ((0,), (0,)), bf16),
        ],
    )
    down_grad, head_part = tie(down_grad, head_part)
    down_part = reduce_to(down_grad, 1)
    second_grad, down_part = tie(second_grad, down_part)
    gateup_part = reduce_to(gateup_w, 0)
    middle_extra, middle_gain = norm_back(middle_rows, gains_rows[1], second_grad)
    residual = residual + middle_extra

    branch = residual.astype(bf16)
    place = lax.axis_index("dp")
    by_owner = branch.reshape(home, n_dp // 2, 2, table_cols)

    def columns_for(parity):
        return lax.dynamic_index_in_dim(by_owner, parity, 2, False).reshape(home, -1)

    given = dot(mixed, columns_for(1 - place % 2), ((0,), (0,)), bf16)
    kept = dot(mixed, columns_for(place % 2), ((0,), (0,)), bf16)
    branch, (given, kept) = tie(branch, (given, kept))
    taken = lax.ppermute(given, "dp", [(k, k ^ 1) for k in range(n_dp)])

    def owner_columns(hop):
        at = ((place // 2) ^ hop) * table_cols
        return (
            lax.dynamic_slice_in_dim(kept, at, table_cols, 1).astype(f32)
            + lax.dynamic_slice_in_dim(taken, at, table_cols, 1).astype(f32)
        )

    output_w = [owner_columns(0)]
    for hop in range(1, n_dp // 2):
        output_w.append(
            lax.ppermute(
                owner_columns(hop).astype(bf16), "dp", [(k, k ^ (2 * hop)) for k in range(n_dp)]
            )
        )
    mixed_grad = dot(branch, output_full, ((1,), (1,)), bf16)
    query_pre, kv_grad = attend_back(rope, kv, lse, mixed_grad, cosine, sine, places, key_places)
    kv_halves = kv_grad.reshape(2, n_mp, strip, kv_cols)
    kv_grad = ring_scatter([jnp.concatenate([kv_halves[0, i], kv_halves[1, i]]) for i in range(n_mp)])
    pair_grad = turn_keys(kv_grad, cosine, sine, -1.0, KVH)
    kvq_grad = jnp.concatenate([pair_grad, query_pre], 1)
    kv_own = kv_cols // n_mp

    def piece_columns(hop):
        there = (group - hop) % n_mp
        return jnp.concatenate(
            [
                lax.dynamic_slice_in_dim(kvq_grad, there * kv_own, kv_own, 1),
                lax.dynamic_slice_in_dim(kvq_grad, kv_cols + there * q_cols, q_cols, 1),
            ],
            1,
        )

    columns = {0: piece_columns(0)}
    for hop in range(1, n_mp):
        columns[n_mp - hop] = ring(piece_columns(hop), -hop)
    columns = jnp.concatenate([columns[i] for i in piece_order()])
    kvq_w = dot(first_all, columns, ((0,), (0,)), bf16)
    first_grad = dot(kvq_grad, kvq_full, ((1,), (1,)))
    start_extra, start_gain = norm_back(start_rows, gains_rows[0], first_grad)
    start_grad = (residual + start_extra).astype(bf16)
    gains_grad = jnp.stack([start_gain, middle_gain, final_gain]).astype(bf16)

    def piece_of(x, hop, axis, length):
        return lax.dynamic_slice_in_dim(x, (group - hop) % n_mp * length, length, axis)

    moved = jnp.concatenate([start_grad, gains_grad, jnp.zeros((13, start_grad.shape[1]), bf16)])
    moved = moved.reshape(-1, n_dp, table_cols).transpose(1, 0, 2)
    moved = lax.all_to_all(moved, "dp", 0, 0)
    moved, kvq_w = tie(moved, kvq_w)
    kvq_w, gateup_part = tie(kvq_w, gateup_part)
    kvq_w = reduce_to(kvq_w, 0)
    gateup_part = gateup_part.reshape(table_cols, 2, half).transpose(1, 0, 2)
    gains_part = ring_scatter([jnp.sum(moved[:, home : home + 3].astype(f32), 0)] * n_mp)
    embed_part = None
    ids_home = by_piece(ids, jnp.arange(n_mp)).transpose(1, 0, 2).reshape(n_mp, -1) - vocab_start
    for number, (device, shard) in enumerate(
        arrivals(moved[:, :home].reshape(n_dp * home, table_cols))
    ):
        onehot = (ids_home[device][None, :] == jnp.arange(table_rows)[:, None]).astype(bf16)
        part = dot(onehot, shard)
        embed_part = part if embed_part is None else embed_part + part
        if number == n_mp // 2:
            output_w, embed_part = tie(output_w, embed_part)
            output_w = sum(piece.astype(f32) for piece in output_w).astype(bf16)

    query_part = kvq_w[:, kv_own:]
    keyvalue_part = ordered(ring_gather(kvq_w[:, :kv_own]), 1)
    keyvalue_part = keyvalue_part.reshape(-1, KVH, 2, HD).transpose(0, 2, 1, 3).reshape(-1, kv_cols)
    output_part = ring_scatter(
        [piece_of(output_w, i, 0, output_weight.shape[0]) for i in range(n_mp)]
    )

    leading = (group == 0).astype(f32)

    def square(piece):
        piece = piece.astype(f32)
        return jnp.sum(piece * piece)

    squared = sum(
        square(piece)
        for piece in (embed_part, query_part, output_part, gateup_part, down_part, head_part)
    )
    squared = squared + leading * (square(keyvalue_part) + square(gains_part))
    totals = jnp.stack([squared, loss_part])[:, None]
    totals = sum(ring_gather(totals))
    hop = 1
    while hop < n_dp:
        totals = totals + lax.ppermute(totals, "dp", [(k, k ^ hop) for k in range(n_dp)])
        hop *= 2
    grad_norm, loss_sum = jnp.sqrt(totals[0, 0]), totals[1, 0]
    factor = jnp.minimum(1.0, CLIP / (grad_norm + 1e-06))
    outs = [loss_sum, weight_total, grad_norm]
    for number, (weight, grad, mean_old, square_old) in enumerate(
        (
            (embed_table, embed_part, embed_mean, embed_square),
            (query_weight, query_part, query_mean, query_square),
            (keyvalue_weight, keyvalue_part, keyvalue_mean, keyvalue_square),
            (output_weight, output_part, output_mean, output_square),
            (gateup_weight, gateup_part, gateup_mean, gateup_square),
            (down_weight, down_part, down_mean, down_square),
            (head_weight, head_part, head_mean, head_square),
            (norm_gains, gains_part, gains_mean, gains_square),
        )
    ):
        new, mean_new, square_new = adamw(
            weight, grad, mean_old, square_old, factor, RATES[number], DECAYS[number]
        )
        outs += [new, embed_part * factor if number == 0 else mean_new, square_new]
    return tuple(outs)


def solution(mesh):
    weights = (
        P("mp", "dp"),
        P("dp", "mp"),
        P("dp", None),
        P("mp", "dp"),
        P(None, "dp", "mp"),
        P("mp", "dp"),
        P("dp", "mp"),
        P(None, "dp"),
    )
    in_specs = (P("dp"),) * 4 + weights * 3
    out_specs = (P(),) * 3 + tuple(spec for spec in weights for _ in range(3))
    return jax.shard_map(body, mesh=mesh, in_specs=in_specs, out_specs=out_specs, check_vma=False)
```
